32 devices in a mesh: groups: 2 (over x), shot: 16 (over z, y, core).
Axes of the slice: x: 2, y: 2, z: 4, core: 2. Of those that a mesh axis runs over, the one named last changes fastest.
Arguments:
- forward_state: float32 [32, 13, 16, 64, 128], P(('groups', 'shot')), parts along dimension 0, may hold values from -6 to 6
- adjoint_state: float32 [32, 13, 16, 64, 128], P(('groups', 'shot')), parts along dimension 0, may hold values from -6 to 6
- source_amp: float32 [32, 2], P(('groups', 'shot')), parts along dimension 0, may hold values from -12 to 12
- source_cell: int32 [32], P(('groups', 'shot')), parts along dimension 0, may hold values from 0 to 131071
- receiver_cells: int32 [32, 1024], P(('groups', 'shot')), parts along dimension 0, may hold values from 0 to 131071
- recorded: float32 [32, 1024], P(('groups', 'shot')), parts along dimension 0, may hold values from -6 to 6
- material: float32 [4, 32, 64, 128], P(None, 'groups', 'shot'), parts along dimension 1, may hold values from 0.3 to 2
- cell_class: int32 [32, 64, 128], P('groups'), parts along dimension 0, may hold values from 0 to 3
- class_factors: float32 [4, 4], replicated, may hold values from 0.5 to 2
Outputs:
- gradient: float32 [4, 32, 64, 128], P(None, 'groups', 'shot'), parts along dimension 1
The draws below stay inside these ranges and needn't reach their ends.
There are 2 independent parts, one for each index of `groups`. The reference program is written for one: setup_inputs(seed, part) draws one part's arguments, and reference() takes and returns one part's arrays. A program takes and returns all parts, laid end to end along the dimension named above; an argument that names none is the same for every part. Nothing has to cross between parts.
All inputs are finite; a program needn't handle non-finite values.
Results may differ from the reference program's by a relative error of at most 0.00002.
Values sent between devices are 32-bit elements; how exact they have to be, the bound alone decides.
No kernel may reach another device: no remote copies, remote signals or barrier semaphores. Data moves between devices by JAX's collectives and lax.ppermute only.
A program may use at most 128 MiB of HBM per device.

```python
import math
import jax
import jax.numpy as jnp
from jax import lax

PLANES = 16
NZ = 64
NY = 128
NREC = 1024
NCLASS = 4
SHOTS = 16
CELLS = 131072


def with_ends(drawn, rng, low, top_value):
    index_at = [jax.random.randint(jax.random.fold_in(rng, axis), (), 0, length) for axis, length in enumerate(drawn.shape)]
    longest = drawn.shape.index(max(drawn.shape))
    neighbour = index_at[:longest] + [(index_at[longest] + 1) % drawn.shape[longest]] + index_at[longest + 1:]
    return drawn.at[tuple(index_at)].set(low).at[tuple(neighbour)].set(top_value)


def block_levels(key, extent, cuts, least, high):
    factor_of, own = 1.0, jax.random.fold_in(key, 6)
    for position, blocks in cuts:
        draws = jnp.exp(jax.random.uniform(jax.random.fold_in(own, position), (blocks,), jnp.float32, least / len(cuts), high / len(cuts)))
        factor_of = factor_of * jnp.repeat(draws, extent[position] // blocks).reshape([-1 if axis == position else 1 for axis in range(len(extent))])
    return factor_of


def gaussian(key, dims, scale, reach, cuts=(), held_as=jnp.bfloat16):
    result = scale * jax.random.normal(key, dims, jnp.float32)
    if cuts:
        result = result * block_levels(key, dims, cuts, -0.22, 0.18)
    return jnp.clip(result, -reach, reach).astype(held_as)


def setup_inputs(seed: int = 0, part: int = 0) -> dict:
    seeds = jax.random.split(jax.random.key(seed), 10)
    part_keys = jax.random.split(jax.random.fold_in(seeds[9], part), 10)
    return {
        "forward_state": gaussian(part_keys[0], (SHOTS, 13, PLANES, NZ, NY), 1.0, 6.0, ((0, 16),), jnp.float32),
        "adjoint_state": gaussian(part_keys[1], (SHOTS, 13, PLANES, NZ, NY), 1.0, 6.0, ((0, 16),), jnp.float32),
        "source_amp": gaussian(part_keys[2], (SHOTS, 2), 3.0, 12.0, ((0, 16),), jnp.float32),
        "source_cell": with_ends(jax.random.randint(part_keys[3], (SHOTS,), 0, CELLS), jax.random.fold_in(part_keys[3], 1), 0, CELLS - 1).astype(jnp.int32),
        "receiver_cells": with_ends(jax.random.randint(part_keys[4], (SHOTS, NREC), 0, CELLS), jax.random.fold_in(part_keys[4], 1), 0, CELLS - 1).astype(jnp.int32),
        "recorded": gaussian(part_keys[5], (SHOTS, NREC), 1.0, 6.0, ((0, 16),), jnp.float32),
        "material": jnp.clip(jnp.exp(math.log(2.0) - 1.89712 * jax.random.uniform(part_keys[6], (4, PLANES, NZ, NY), jnp.float32) ** block_levels(part_keys[6], (4, PLANES, NZ, NY), ((2, 16),), -0.2, 0.2)), 0.3, 2.0),
        "cell_class": with_ends(jax.random.randint(part_keys[7], (PLANES, NZ, NY), 0, NCLASS), jax.random.fold_in(part_keys[7], 1), 0, NCLASS - 1).astype(jnp.int32),
        "class_factors": jnp.clip(jnp.exp(jax.random.uniform(seeds[8], (4, NCLASS), jnp.float32, math.log(0.5), math.log(2.0))), 0.5, 2.0),
    }


BIOT_COEFF = 0.8
RHO_BULK = 2.2
RHO_FLUID = 1.0
MASS_FLUID = 2.5
TIME_STEP = 0.25

def forward_diff(field, axis):
    count = field.shape[axis]
    ahead = jnp.concatenate([lax.slice_in_dim(field, 1, count, axis=axis), jnp.zeros_like(lax.slice_in_dim(field, 0, 1, axis=axis))], axis=axis)
    return ahead - field

def backward_diff(field, axis):
    count = field.shape[axis]
    behind = jnp.concatenate([jnp.zeros_like(lax.slice_in_dim(field, 0, 1, axis=axis)), lax.slice_in_dim(field, 0, count - 1, axis=axis)], axis=axis)
    return field - behind

def advance(state, model, amplitude, source):
    vel_x, vel_z, vel_y, flux_x, flux_z, flux_y = (state[0], state[1], state[2], state[3], state[4], state[5])
    sig_xx, sig_zz, sig_yy, sig_xz, sig_xy, sig_zy, pressure = (state[6], state[7], state[8], state[9], state[10], state[11], state[12])
    lame_first, shear_mod, biot_mod, damping = (model[0], model[1], model[2], model[3])
    determinant = RHO_BULK * MASS_FLUID - RHO_FLUID * RHO_FLUID
    force_x = forward_diff(sig_xx, 0) + backward_diff(sig_xz, 1) + backward_diff(sig_xy, 2)
    force_z = backward_diff(sig_xz, 0) + forward_diff(sig_zz, 1) + backward_diff(sig_zy, 2)
    force_y = backward_diff(sig_xy, 0) + backward_diff(sig_zy, 1) + forward_diff(sig_yy, 2)
    drag_x = -forward_diff(pressure, 0) - damping * flux_x
    drag_z = -forward_diff(pressure, 1) - damping * flux_z
    drag_y = -forward_diff(pressure, 2) - damping * flux_y
    vel_x = vel_x + TIME_STEP * (MASS_FLUID * force_x - RHO_FLUID * drag_x) / determinant
    vel_z = vel_z + TIME_STEP * (MASS_FLUID * force_z - RHO_FLUID * drag_z) / determinant
    vel_y = vel_y + TIME_STEP * (MASS_FLUID * force_y - RHO_FLUID * drag_y) / determinant
    flux_x = flux_x + TIME_STEP * (RHO_BULK * drag_x - RHO_FLUID * force_x) / determinant
    flux_z = flux_z + TIME_STEP * (RHO_BULK * drag_z - RHO_FLUID * force_z) / determinant
    flux_y = flux_y + TIME_STEP * (RHO_BULK * drag_y - RHO_FLUID * force_y) / determinant
    strain_xx = backward_diff(vel_x, 0)
    strain_zz = backward_diff(vel_z, 1)
    strain_yy = backward_diff(vel_y, 2)
    div_solid = strain_xx + strain_zz + strain_yy
    div_flux = backward_diff(flux_x, 0) + backward_diff(flux_z, 1) + backward_diff(flux_y, 2)
    strain_xz = 0.5 * (forward_diff(vel_x, 1) + forward_diff(vel_z, 0))
    strain_xy = 0.5 * (forward_diff(vel_x, 2) + forward_diff(vel_y, 0))
    strain_zy = 0.5 * (forward_diff(vel_z, 2) + forward_diff(vel_y, 1))
    bulk_term = (lame_first + BIOT_COEFF * BIOT_COEFF * biot_mod) * div_solid + BIOT_COEFF * biot_mod * div_flux
    sig_xx = sig_xx + TIME_STEP * (2.0 * shear_mod * strain_xx + bulk_term)
    sig_zz = sig_zz + TIME_STEP * (2.0 * shear_mod * strain_zz + bulk_term)
    sig_yy = sig_yy + TIME_STEP * (2.0 * shear_mod * strain_yy + bulk_term)
    sig_xz = sig_xz + TIME_STEP * 2.0 * shear_mod * strain_xz
    sig_xy = sig_xy + TIME_STEP * 2.0 * shear_mod * strain_xy
    sig_zy = sig_zy + TIME_STEP * 2.0 * shear_mod * strain_zy
    pressure = pressure - TIME_STEP * biot_mod * (BIOT_COEFF * div_solid + div_flux)
    pressure = pressure.reshape(-1).at[source].add(amplitude).reshape(pressure.shape)
    return jnp.stack([vel_x, vel_z, vel_y, flux_x, flux_z, flux_y, sig_xx, sig_zz, sig_yy, sig_xz, sig_xy, sig_zy, pressure])

def shot_gradient(model, start_state, adjoint, amplitudes, source, receivers, observed):

    def march(params):
        state = start_state
        for section in range(2):
            state = advance(state, params, amplitudes[section], source)
        return state
    final, pullback = jax.vjp(march, model)
    misfit = final[12].reshape(-1)[receivers] - observed
    pressure_cot = adjoint[12].reshape(-1).at[receivers].add(misfit).reshape(adjoint[12].shape)
    cotangent = adjoint.at[12].set(pressure_cot)
    return pullback(cotangent)[0]

def class_factor_map(cell_class, class_factors):
    classes = jnp.arange(class_factors.shape[1], dtype=jnp.int32)
    onehot = (cell_class[None] == classes[:, None, None, None]).astype(jnp.float32)
    return lax.optimization_barrier(jnp.sum(class_factors[:, :, None, None, None] * onehot[None], axis=1))

def reference(forward_state, adjoint_state, source_amp, source_cell, receiver_cells, recorded, material, cell_class, class_factors):
    factor = class_factor_map(cell_class, class_factors)
    model = material * factor

    def accumulate(total, items):
        start_state, adjoint, amplitudes, source, receivers, observed = items
        return (total + shot_gradient(model, start_state, adjoint, amplitudes, source, receivers, observed), None)
    total, unused = lax.scan(accumulate, jnp.zeros_like(material), (forward_state, adjoint_state, source_amp, source_cell, receiver_cells, recorded))
    return total * factor / jnp.sqrt(jnp.float32(SHOTS))
```

```python
import functools

import jax
import jax.numpy as jnp
from jax import lax
from jax.experimental import pallas as pl
from jax.experimental.pallas import tpu as pltpu
from jax.sharding import PartitionSpec as P

ALPHA = 0.8
RHO_BULK = 2.2
RHO_FLUID = 1.0
MASS_FLUID = 2.5
DT = 0.25
DET = RHO_BULK * MASS_FLUID - RHO_FLUID * RHO_FLUID
C1 = DT * MASS_FLUID / DET
C2 = DT * RHO_FLUID / DET
C3 = DT * RHO_BULK / DET

GUARD = 8
F32 = jnp.float32


def shot_kernel(
    me_ref,
    cell_ref,
    amp_ref,
    pieces_ref,
    state_hbm,
    adj_hbm,
    hits_hbm,
    seen_hbm,
    out_ref,
    st,
    q1,
    q2,
    eh,
    fr,
    adj,
    hits,
    seen,
    strain,
    model,
    grad,
    sem_state,
    sem_adj,
    sem_hits,
    *,
    n,
    nx,
    nz,
    ny,
    chunk,
):
    piece = nz // n
    inner = pl.ds(GUARD, nz)

    def state_copy(f):
        return pltpu.make_async_copy(
            state_hbm.at[f], st.at[f, pl.ds(1, nx), inner, :], sem_state.at[f]
        )

    order = (6, 9, 10, 7, 11, 8, 12, 0, 1, 2, 3, 4, 5)
    for f in order:
        state_copy(f).start()
    adj_copy = pltpu.make_async_copy(adj_hbm, adj, sem_adj)
    adj_copy.start()
    hits_copy = pltpu.make_async_copy(hits_hbm, hits, sem_hits.at[0])
    seen_copy = pltpu.make_async_copy(seen_hbm, seen, sem_hits.at[1])
    hits_copy.start()
    seen_copy.start()

    zrow = jnp.zeros((GUARD, ny), F32)

    def guard_fields():
        for f in range(13):
            yield st, f
        for f in range(3):
            yield q1, f
            yield q2, f
        for f in range(7):
            yield eh, f
        for f in range(6):
            yield fr, f

    for ref, f in guard_fields():
        for x in (0, nx + 1):
            for z in range(0, nz + 2 * GUARD, GUARD):
                ref[f, x, z : z + GUARD, :] = zrow

    def zero_rows(x, carry):
        for ref, f in guard_fields():
            ref[f, x, 0:GUARD, :] = zrow
            ref[f, x, nz + GUARD : nz + 2 * GUARD, :] = zrow
        return carry

    lax.fori_loop(1, nx + 1, zero_rows, 0)

    me = me_ref[0]
    starts = [pl.multiple_of((me ^ r) * piece, piece) for r in range(n)]

    def assemble(x, carry):
        for k in range(4):
            for r in range(n):
                model[k, x, pl.ds(starts[r], piece), :] = pieces_ref[
                    r, pl.ds((k * nx + x) * piece, piece), :
                ]
        return carry

    lax.fori_loop(0, nx, assemble, 0)

    for f in order:
        state_copy(f).wait()

    lane = lax.broadcasted_iota(jnp.int32, (chunk, ny), 1)
    first, last = lane == 0, lane == ny - 1
    zero = jnp.zeros((chunk, ny), F32)

    def at(ref, f, x, z, dx=0, dz=0):
        return ref[f, x + 1 + dx, pl.ds(GUARD + z + dz, chunk), :]

    def put(ref, f, x, z, value):
        ref[f, x + 1, pl.ds(GUARD + z, chunk), :] = value

    def ahead(f):
        return jnp.where(last, zero, pltpu.roll(f, ny - 1, 1))

    def behind(f):
        return jnp.where(first, zero, pltpu.roll(f, 1, 1))

    def fwd(ref, f, x, z, axis, here=None):
        here = at(ref, f, x, z) if here is None else here
        if axis == 0:
            return at(ref, f, x, z, dx=1) - here
        if axis == 1:
            return at(ref, f, x, z, dz=1) - here
        return ahead(here) - here

    def bwd(ref, f, x, z, axis, here=None):
        here = at(ref, f, x, z) if here is None else here
        if axis == 0:
            return here - at(ref, f, x, z, dx=-1)
        if axis == 1:
            return here - at(ref, f, x, z, dz=-1)
        return here - behind(here)

    def over_cells(body):
        def plane(x, carry):
            for z in range(0, nz, chunk):
                body(x, z)
            return carry

        lax.fori_loop(0, nx, plane, 0)

    def mod(k, x, z):
        return model[k, x, pl.ds(z, chunk), :]

    def forces(x, z):
        sxx, szz, syy, sxz, sxy, szy, p = [at(st, 6 + i, x, z) for i in range(7)]
        fx = fwd(st, 6, x, z, 0, sxx) + bwd(st, 9, x, z, 1, sxz) + bwd(st, 10, x, z, 2, sxy)
        fz = bwd(st, 9, x, z, 0, sxz) + fwd(st, 7, x, z, 1, szz) + bwd(st, 11, x, z, 2, szy)
        fy = bwd(st, 10, x, z, 0, sxy) + bwd(st, 11, x, z, 1, szy) + fwd(st, 8, x, z, 2, syy)
        g = [fwd(st, 12, x, z, d, p) for d in range(3)]
        return (fx, fz, fy), g

    def velocities(x, z, q_from, q_at, q_to):
        f, g = forces(x, z)
        damp = mod(3, x, z)
        for d in range(3):
            q = at(q_from, q_at + d, x, z)
            drag = g[d] + damp * q
            put(st, d, x, z, at(st, d, x, z) + (C1 * f[d] + C2 * drag))
            put(q_to, d, x, z, q - (C3 * drag + C2 * f[d]))

    def strains(x, z, q):
        vx, vz, vy = [at(st, i, x, z) for i in range(3)]
        exx = bwd(st, 0, x, z, 0, vx)
        ezz = bwd(st, 1, x, z, 1, vz)
        eyy = bwd(st, 2, x, z, 2, vy)
        dq = bwd(q, 0, x, z, 0) + bwd(q, 1, x, z, 1) + bwd(q, 2, x, z, 2)
        hxz = fwd(st, 0, x, z, 1, vx) + fwd(st, 1, x, z, 0, vz)
        hxy = fwd(st, 0, x, z, 2, vx) + fwd(st, 2, x, z, 0, vy)
        hzy = fwd(st, 1, x, z, 2, vz) + fwd(st, 2, x, z, 1, vy)
        dv = exx + ezz + eyy
        w = ALPHA * dv + dq
        return exx, ezz, eyy, hxz, hxy, hzy, dv, w

    over_cells(lambda x, z: velocities(x, z, st, 3, q1))

    def stresses(x, z):
        exx, ezz, eyy, hxz, hxy, hzy, dv, w = strains(x, z, q1)
        lame, shear, biot = [DT * mod(k, x, z) for k in range(3)]
        bw = biot * w
        bulk = lame * dv + ALPHA * bw
        shear2 = 2.0 * shear
        for i, e in enumerate((exx, ezz, eyy)):
            put(st, 6 + i, x, z, at(st, 6 + i, x, z) + (shear2 * e + bulk))
        for i, h in enumerate((hxz, hxy, hzy)):
            put(st, 9 + i, x, z, at(st, 9 + i, x, z) + shear * h)
        put(st, 12, x, z, at(st, 12, x, z) - bw)
        for i, e in enumerate((exx, ezz, eyy, hxz, hxy, hzy, w)):
            strain[i, x, pl.ds(z, chunk), :] = e

    over_cells(stresses)

    cell = cell_ref[0]
    src_x, src_z, src_y = cell // (nz * ny), (cell // ny) % nz, cell % ny
    src_lane = lax.broadcasted_iota(jnp.int32, (1, ny), 1) == src_y
    row = st[12, src_x + 1, pl.ds(GUARD + src_z, 1), :]
    st[12, src_x + 1, pl.ds(GUARD + src_z, 1), :] = row + jnp.where(src_lane, amp_ref[0], 0.0)

    over_cells(lambda x, z: velocities(x, z, q1, 0, q2))

    adj_copy.wait()
    hits_copy.wait()
    seen_copy.wait()

    row = hits[src_x, pl.ds(src_z, 1), :]
    prow = adj[12, src_x, pl.ds(src_z, 1), :]
    adj[12, src_x, pl.ds(src_z, 1), :] = prow + jnp.where(src_lane, row * amp_ref[1], 0.0)

    def adj_at(f, x, z):
        return adj[f, x, pl.ds(z, chunk), :]

    def correlate(x, z, e, h, w, s, p, first_time):
        lame, shear, biot = [DT * mod(k, x, z) for k in range(3)]
        trace = s[0] + s[1] + s[2]
        dv = e[0] + e[1] + e[2]
        load = ALPHA * trace - p
        diag = s[0] * e[0] + s[1] * e[1] + s[2] * e[2]
        off = s[3] * h[0] + s[4] * h[1] + s[5] * h[2]
        for k, value in enumerate((trace * dv, 2.0 * diag + off, load * w)):
            value = DT * value
            if not first_time:
                value = grad[k, x, pl.ds(z, chunk), :] + value
            grad[k, x, pl.ds(z, chunk), :] = value
        t = biot * load
        bulk = lame * trace + ALPHA * t
        shear2 = 2.0 * shear
        for i in range(3):
            put(eh, i, x, z, shear2 * s[i] + bulk)
        for i in range(3):
            put(eh, 3 + i, x, z, shear * s[3 + i])
        put(eh, 6, x, z, t)

    def stress_back_2(x, z):
        exx, ezz, eyy, hxz, hxy, hzy, dv, w = strains(x, z, q2)
        final_p = at(st, 12, x, z) - DT * mod(2, x, z) * w
        s = [adj_at(6 + i, x, z) for i in range(6)]
        p = adj_at(12, x, z) + (hits[x, pl.ds(z, chunk), :] * final_p - seen[x, pl.ds(z, chunk), :])
        adj[12, x, pl.ds(z, chunk), :] = p
        correlate(x, z, (exx, ezz, eyy), (hxz, hxy, hzy), w, s, p, True)

    over_cells(stress_back_2)

    def velocity_bars(x, z, v, q):
        ex, ez, ey, hxz, hxy, hzy, t = [at(eh, i, x, z) for i in range(7)]
        vx = v[0] - (fwd(eh, 0, x, z, 0, ex) + bwd(eh, 3, x, z, 1, hxz) + bwd(eh, 4, x, z, 2, hxy))
        vz = v[1] - (bwd(eh, 3, x, z, 0, hxz) + fwd(eh, 1, x, z, 1, ez) + bwd(eh, 5, x, z, 2, hzy))
        vy = v[2] - (bwd(eh, 4, x, z, 0, hxy) + bwd(eh, 5, x, z, 1, hzy) + fwd(eh, 2, x, z, 2, ey))
        qs = [q[d] - fwd(eh, 6, x, z, d, t) for d in range(3)]
        return (vx, vz, vy), qs

    def velocity_back_2(x, z):
        v, q = velocity_bars(
            x, z, [adj_at(d, x, z) for d in range(3)], [adj_at(3 + d, x, z) for d in range(3)]
        )
        damp = mod(3, x, z)
        total = zero
        for d in range(3):
            r = C3 * q[d] - C2 * v[d]
            put(fr, d, x, z, C1 * v[d] - C2 * q[d])
            put(fr, 3 + d, x, z, r)
            total = total + at(q1, d, x, z) * r
            adj[d, x, pl.ds(z, chunk), :] = v[d]
            adj[3 + d, x, pl.ds(z, chunk), :] = q[d] - damp * r
        grad[3, x, pl.ds(z, chunk), :] = total

    over_cells(velocity_back_2)

    def stress_back_1(x, z):
        fx, fz, fy = [at(fr, i, x, z) for i in range(3)]
        s = [
            adj_at(6, x, z) - bwd(fr, 0, x, z, 0, fx),
            adj_at(7, x, z) - bwd(fr, 1, x, z, 1, fz),
            adj_at(8, x, z) - bwd(fr, 2, x, z, 2, fy),
            adj_at(9, x, z) - (fwd(fr, 0, x, z, 1, fx) + fwd(fr, 1, x, z, 0, fz)),
            adj_at(10, x, z) - (fwd(fr, 0, x, z, 2, fx) + fwd(fr, 2, x, z, 0, fy)),
            adj_at(11, x, z) - (fwd(fr, 1, x, z, 2, fz) + fwd(fr, 2, x, z, 1, fy)),
        ]
        p = adj_at(12, x, z) + (
            bwd(fr, 3, x, z, 0) + bwd(fr, 4, x, z, 1) + bwd(fr, 5, x, z, 2)
        )
        e = [strain[i, x, pl.ds(z, chunk), :] for i in range(7)]
        correlate(x, z, e[0:3], e[3:6], e[6], s, p, False)

    over_cells(stress_back_1)

    def velocity_back_1(x, z):
        v, q = velocity_bars(
            x, z, [adj_at(d, x, z) for d in range(3)], [adj_at(3 + d, x, z) for d in range(3)]
        )
        total = grad[3, x, pl.ds(z, chunk), :]
        for d in range(3):
            total = total + at(st, 3 + d, x, z) * (C3 * q[d] - C2 * v[d])
        grad[3, x, pl.ds(z, chunk), :] = -total

    over_cells(velocity_back_1)

    def split(x, carry):
        for k in range(4):
            for r in range(n):
                out_ref[r, pl.ds((k * nx + x) * piece, piece), :] = grad[
                    k, x, pl.ds(starts[r], piece), :
                ]
        return carry

    lax.fori_loop(0, nx, split, 0)


def shot_gradient(me, cell, amps, pieces, state, adjoint, hits, seen, n):
    nf, nx, nz, ny = state.shape
    padded = (nx + 2, nz + 2 * GUARD, ny)
    smem = pl.BlockSpec(memory_space=pltpu.SMEM)
    vmem = pl.BlockSpec(memory_space=pltpu.VMEM)
    hbm = pl.BlockSpec(memory_space=pltpu.HBM)
    cells = (nx, nz, ny)
    return pl.pallas_call(
        functools.partial(shot_kernel, n=n, nx=nx, nz=nz, ny=ny, chunk=16),
        out_shape=jax.ShapeDtypeStruct(pieces.shape, F32),
        in_specs=[smem, smem, smem, vmem, hbm, hbm, hbm, hbm],
        out_specs=vmem,
        scratch_shapes=[
            pltpu.VMEM((nf, *padded), F32),
            pltpu.VMEM((3, *padded), F32),
            pltpu.VMEM((3, *padded), F32),
            pltpu.VMEM((7, *padded), F32),
            pltpu.VMEM((6, *padded), F32),
            pltpu.VMEM((nf, *cells), F32),
            pltpu.VMEM(cells, F32),
            pltpu.VMEM(cells, F32),
            pltpu.VMEM((7, *cells), F32),
            pltpu.VMEM((4, *cells), F32),
            pltpu.VMEM((4, *cells), F32),
            pltpu.SemaphoreType.DMA((nf,)),
            pltpu.SemaphoreType.DMA,
            pltpu.SemaphoreType.DMA((2,)),
        ],
        compiler_params=pltpu.CompilerParams(vmem_limit_bytes=60 * 1024 * 1024),
        cost_estimate=pl.CostEstimate(
            flops=600 * nx * nz * ny, bytes_accessed=30 * nx * nz * ny * 4, transcendentals=0
        ),
        name="shot",
    )(me, cell, amps, pieces, state, adjoint, hits, seen)


def receiver_kernel(cell_ref, rec_ref, hits_ref, seen_ref, *, count, ny):
    hits_ref[...] = jnp.zeros_like(hits_ref)
    seen_ref[...] = jnp.zeros_like(seen_ref)
    lane = lax.broadcasted_iota(jnp.int32, (1, ny), 1)

    def add(i, carry):
        cell = cell_ref[0, i]
        here = lane == cell % ny
        row = pl.ds(cell // ny, 1)
        hits_ref[row, :] += jnp.where(here, 1.0, 0.0)
        seen_ref[row, :] += jnp.where(here, rec_ref[0, i], 0.0)
        return carry

    lax.fori_loop(0, count, add, 0)


def receiver_maps(receivers, recorded, nx, nz, ny):
    smem = pl.BlockSpec(memory_space=pltpu.SMEM)
    vmem = pl.BlockSpec(memory_space=pltpu.VMEM)
    count = receivers.shape[1]
    shape = jax.ShapeDtypeStruct((nx * nz, ny), F32)
    hits, seen = pl.pallas_call(
        functools.partial(receiver_kernel, count=count, ny=ny),
        out_shape=(shape, shape),
        in_specs=[smem, smem],
        out_specs=(vmem, vmem),
        cost_estimate=pl.CostEstimate(
            flops=nx * nz * ny * 40, bytes_accessed=2 * nx * nz * ny * 4, transcendentals=0
        ),
        name="receivers",
    )(receivers, recorded)
    return hits.reshape(nx, nz, ny), seen.reshape(nx, nz, ny)


def partner(x, bit, n):
    return lax.ppermute(x, "shot", [(i, i ^ bit) for i in range(n)])


def gather_pieces(own, n):
    far = [partner(own, b, n) for b in range(4, n, 4)]
    line = jnp.stack([own, *far])
    both = jnp.stack([line, partner(line, 2, n)], axis=1)
    whole = jnp.stack([both, partner(both, 1, n)], axis=2)
    return whole.reshape(n, *own.shape)


def scatter_sum(pieces, n):
    kept = pieces[0::2] + partner(pieces[1::2], 1, n)
    kept = kept[0::2] + partner(kept[1::2], 2, n)
    total = kept[0]
    for i in range(1, n // 4):
        total = total + partner(kept[i], 4 * i, n)
    return total


def per_device(
    forward_state,
    adjoint_state,
    source_amp,
    source_cell,
    receiver_cells,
    recorded,
    material,
    cell_class,
    class_factors,
):
    n = lax.axis_size("shot")
    me = lax.axis_index("shot")
    _, nx, piece, ny = material.shape
    nz = cell_class.shape[1]
    own_class = lax.dynamic_slice_in_dim(cell_class, me * piece, piece, 1)
    factor = jnp.zeros_like(material)
    for c in range(class_factors.shape[1]):
        factor = jnp.where(own_class[None] == c, class_factors[:, c, None, None, None], factor)
    own = (material * factor).reshape(-1, ny)
    pieces = gather_pieces(own, n)
    hits, seen = receiver_maps(receiver_cells, recorded, nx, nz, ny)
    parts = shot_gradient(
        me.reshape(1),
        source_cell,
        source_amp[0],
        pieces,
        forward_state[0],
        adjoint_state[0],
        hits,
        seen,
        n,
    )
    summed = scatter_sum(parts, n).reshape(material.shape)
    return summed * factor / jnp.sqrt(jnp.float32(forward_state.shape[0] * n))


def solution(mesh):
    placed = (
        P(("groups", "shot"), None, None, None, None),
        P(("groups", "shot"), None, None, None, None),
        P(("groups", "shot"), None),
        P(("groups", "shot")),
        P(("groups", "shot"), None),
        P(("groups", "shot"), None),
        P(None, "groups", "shot", None),
        P("groups", None, None),
        P(),
    )
    return jax.shard_map(
        per_device,
        mesh=mesh,
        in_specs=placed,
        out_specs=P(None, "groups", "shot", None),
        check_vma=False,
    )
```

```python
import functools

import jax
import jax.numpy as jnp
from jax import lax
from jax.experimental import pallas as pl
from jax.experimental.pallas import tpu as pltpu
from jax.sharding import PartitionSpec as P

ALPHA = 0.8
RHO_BULK = 2.2
RHO_FLUID = 1.0
MASS_FLUID = 2.5
DT = 0.25
DET = RHO_BULK * MASS_FLUID - RHO_FLUID * RHO_FLUID
C1 = DT * MASS_FLUID / DET
C2 = DT * RHO_FLUID / DET
C3 = DT * RHO_BULK / DET

GUARD = 8
CHUNK = 16
F32 = jnp.float32
BF16 = jnp.bfloat16
PARAMS = pltpu.CompilerParams(vmem_limit_bytes=12 * 1024 * 1024)
SMEM = pl.BlockSpec(memory_space=pltpu.SMEM)
VMEM = pl.BlockSpec(memory_space=pltpu.VMEM)
HBM = pl.BlockSpec(memory_space=pltpu.HBM)

RESIDENT = (
    ("st", 13, True),
    ("q1", 3, True),
    ("q2", 3, True),
    ("eh", 7, True),
    ("fr", 6, True),
    ("adj", 13, False),
    ("hits", 1, False),
    ("seen", 1, False),
    ("strain", 7, False),
    ("model", 4, False),
    ("grad", 4, False),
)
NAMES = tuple(name for name, _, _ in RESIDENT)


def in_vmem(x):
    return pltpu.with_memory_space_constraint(x, pltpu.VMEM)


def in_hbm(x):
    return pltpu.with_memory_space_constraint(x, pltpu.HBM)


def cost(cells, ops):
    return pl.CostEstimate(flops=cells * ops, bytes_accessed=cells * 4, transcendentals=0)


def own_kernel(me_ref, class_factors, classes, material, factor, *owns):
    _, nx, piece, ny = material.shape
    nx_part = nx // len(owns)
    rows = pl.ds(pl.multiple_of(me_ref[0] * piece, piece), piece)
    table = [[class_factors[k, c] for c in range(class_factors.shape[1])] for k in range(4)]
    for x in range(nx):
        which = classes[x, rows, :]
        for k in range(4):
            f = jnp.full((piece, ny), table[k][0], F32)
            for c in range(1, len(table[k])):
                f = jnp.where(which == c, table[k][c], f)
            factor[k, x] = f
            at = (k * nx_part + x % nx_part) * piece
            owns[x // nx_part][at : at + piece, :] = f * material[k, x]


def own_model(me, class_factors, classes, material, parts):
    _, nx, piece, ny = material.shape
    part = pltpu.VMEM((4 * (nx // parts) * piece, ny), F32)
    return pl.pallas_call(
        own_kernel,
        out_shape=(pltpu.VMEM(material.shape, F32), *[part] * parts),
        in_specs=[SMEM, SMEM, VMEM, VMEM],
        out_specs=(VMEM,) * (parts + 1),
        compiler_params=PARAMS,
        cost_estimate=cost(4 * nx * piece * ny, 10),
        name="own_model",
    )(me, class_factors, classes, material)


def load_kernel(src_cell, amp_ref, cell_ref, rec_ref, state_hbm, adj_hbm, *refs):
    sem_state, sem_adj = refs[len(RESIDENT) :]
    r = dict(zip(NAMES, refs))
    nf, nx, nz, ny = state_hbm.shape
    st, adj, hits, seen = r["st"], r["adj"], r["hits"], r["seen"]
    copies = [
        pltpu.make_async_copy(
            state_hbm.at[f], st.at[f, pl.ds(1, nx), pl.ds(GUARD, nz), :], sem_state.at[f]
        )
        for f in range(nf)
    ]
    copies.append(pltpu.make_async_copy(adj_hbm, adj, sem_adj))
    for copy in copies:
        copy.start()

    zrow = jnp.zeros((GUARD, ny), F32)
    padded = [(r[name], f) for name, count, pad in RESIDENT if pad for f in range(count)]

    def zero_rows(x, carry):
        for ref, f in padded:
            ref[f, x, 0:GUARD, :] = zrow
            ref[f, x, nz + GUARD : nz + 2 * GUARD, :] = zrow
        return carry

    lax.fori_loop(0, nx + 2, zero_rows, 0)
    for ref, f in padded:
        for x in (0, nx + 1):
            for z in range(GUARD, nz + GUARD, GUARD):
                ref[f, x, z : z + GUARD, :] = zrow

    cell, rec = cell_ref[...], rec_ref[...]
    count = cell.shape[1]
    row = lax.div(cell, ny)
    lane = cell - row * ny
    high = rec.astype(BF16).astype(F32)
    middle = (rec - high).astype(BF16).astype(F32)
    low = rec - high - middle
    match = lax.broadcasted_iota(jnp.int32, (ny, count), 0) == lane
    columns = jnp.concatenate(
        [jnp.where(match, v, 0.0).astype(BF16) for v in (jnp.ones_like(rec), high, middle, low)], 0
    )
    block = 128
    for b in range(0, nx * nz, block):
        rows = lax.broadcasted_iota(jnp.int32, (block, count), 0) + b == row
        out = lax.dot_general(
            jnp.where(rows, 1.0, 0.0).astype(BF16),
            columns,
            (((1,), (1,)), ((), ())),
            preferred_element_type=F32,
        )
        total = out[:, ny : 2 * ny] + out[:, 2 * ny : 3 * ny] + out[:, 3 * ny :]
        for z in range(0, block, nz):
            x = (b + z) // nz
            hits[0, x] = out[z : z + nz, :ny]
            seen[0, x] = total[z : z + nz]

    for copy in copies:
        copy.wait()

    src_x, src_z, src_y = place(src_cell[0], nz, ny)
    here = lax.broadcasted_iota(jnp.int32, (1, ny), 1) == src_y
    at = (src_x, pl.ds(src_z, 1), slice(None))
    adj[(12, *at)] += jnp.where(here, hits[(0, *at)] * amp_ref[1], 0.0)


def place(cell, nz, ny):
    return cell // (nz * ny), (cell // ny) % nz, cell % ny


def load_fields(cell, amps, receivers, recorded, state, adjoint):
    nf, nx, nz, ny = state.shape
    shapes = tuple(
        pltpu.VMEM((count, *((nx + 2, nz + 2 * GUARD, ny) if pad else (nx, nz, ny))), F32)
        for _, count, pad in RESIDENT
    )
    return pl.pallas_call(
        load_kernel,
        out_shape=shapes,
        in_specs=[SMEM, SMEM, VMEM, VMEM, HBM, HBM],
        out_specs=(VMEM,) * len(shapes),
        scratch_shapes=[pltpu.SemaphoreType.DMA((nf,)), pltpu.SemaphoreType.DMA],
        compiler_params=PARAMS,
        cost_estimate=cost(nx * nz * ny, 150),
        name="load_fields",
    )(cell, amps, receivers, recorded, in_hbm(state), in_hbm(adjoint))


def march_kernel(me_ref, cell_ref, amp_ref, *refs, n, spans, gathered, summed):
    far = n // 4
    pieces = refs[: far + 3] if gathered else ()
    refs = refs[len(pieces) + len(RESIDENT) :]
    r = dict(zip(NAMES, refs))
    outs = refs[len(RESIDENT) :]
    st, q1, q2, eh, fr, adj, hits, seen, strain, model, grad = [r[name] for name in NAMES]
    _, nx, nz, ny = adj.shape
    piece = nz // n
    me = me_ref[0]

    def rows_of(rel):
        return pl.ds(pl.multiple_of((me ^ rel) * piece, piece), piece)

    if gathered:
        low, high = gathered
        span = high - low

        def assemble(x, carry):
            for k in range(4):
                at = pl.ds((k * span + x) * piece, piece)
                for i in range(far):
                    model[k, low + x, rows_of(4 * i), :] = pieces[i][at, :]
                    for part, rel in ((far, 1), (far + 1, 2), (far + 2, 3)):
                        model[k, low + x, rows_of(4 * i + rel), :] = pieces[part][i, at, :]
            return carry

        lax.fori_loop(0, span, assemble, 0)

    lane = lax.broadcasted_iota(jnp.int32, (CHUNK, ny), 1)
    first, last = lane == 0, lane == ny - 1
    zero = jnp.zeros((CHUNK, ny), F32)
    chunk = CHUNK

    def at(ref, f, x, z, dx=0, dz=0):
        return ref[f, x + 1 + dx, pl.ds(GUARD + z + dz, chunk), :]

    def put(ref, f, x, z, value):
        ref[f, x + 1, pl.ds(GUARD + z, chunk), :] = value

    def ahead(f):
        return jnp.where(last, zero, pltpu.roll(f, ny - 1, 1))

    def behind(f):
        return jnp.where(first, zero, pltpu.roll(f, 1, 1))

    def fwd(ref, f, x, z, axis, here=None):
        here = at(ref, f, x, z) if here is None else here
        if axis == 0:
            return at(ref, f, x, z, dx=1) - here
        if axis == 1:
            return at(ref, f, x, z, dz=1) - here
        return ahead(here) - here

    def bwd(ref, f, x, z, axis, here=None):
        here = at(ref, f, x, z) if here is None else here
        if axis == 0:
            return here - at(ref, f, x, z, dx=-1)
        if axis == 1:
            return here - at(ref, f, x, z, dz=-1)
        return here - behind(here)

    def over_cells(number, body):
        begin, end = spans[number]

        def plane(x, carry):
            for z in range(0, nz, chunk):
                body(x, z)
            return carry

        if end > begin:
            lax.fori_loop(begin, end, plane, 0)

    def mod(k, x, z):
        return model[k, x, pl.ds(z, chunk), :]

    def forces(x, z):
        sxx, szz, syy, sxz, sxy, szy, p = [at(st, 6 + i, x, z) for i in range(7)]
        fx = fwd(st, 6, x, z, 0, sxx) + bwd(st, 9, x, z, 1, sxz) + bwd(st, 10, x, z, 2, sxy)
        fz = bwd(st, 9, x, z, 0, sxz) + fwd(st, 7, x, z, 1, szz) + bwd(st, 11, x, z, 2, szy)
        fy = bwd(st, 10, x, z, 0, sxy) + bwd(st, 11, x, z, 1, szy) + fwd(st, 8, x, z, 2, syy)
        g = [fwd(st, 12, x, z, d, p) for d in range(3)]
        return (fx, fz, fy), g

    def velocities(x, z, q_from, q_at, q_to):
        f, g = forces(x, z)
        damp = mod(3, x, z)
        for d in range(3):
            q = at(q_from, q_at + d, x, z)
            drag = g[d] + damp * q
            put(st, d, x, z, at(st, d, x, z) + (C1 * f[d] + C2 * drag))
            put(q_to, d, x, z, q - (C3 * drag + C2 * f[d]))

    def strains(x, z, q):
        vx, vz, vy = [at(st, i, x, z) for i in range(3)]
        exx = bwd(st, 0, x, z, 0, vx)
        ezz = bwd(st, 1, x, z, 1, vz)
        eyy = bwd(st, 2, x, z, 2, vy)
        dq = bwd(q, 0, x, z, 0) + bwd(q, 1, x, z, 1) + bwd(q, 2, x, z, 2)
        hxz = fwd(st, 0, x, z, 1, vx) + fwd(st, 1, x, z, 0, vz)
        hxy = fwd(st, 0, x, z, 2, vx) + fwd(st, 2, x, z, 0, vy)
        hzy = fwd(st, 1, x, z, 2, vz) + fwd(st, 2, x, z, 1, vy)
        dv = exx + ezz + eyy
        w = ALPHA * dv + dq
        return exx, ezz, eyy, hxz, hxy, hzy, dv, w

    def stresses(x, z):
        exx, ezz, eyy, hxz, hxy, hzy, dv, w = strains(x, z, q1)
        lame, shear, biot = [DT * mod(k, x, z) for k in range(3)]
        bw = biot * w
        bulk = lame * dv + ALPHA * bw
        shear2 = 2.0 * shear
        for i, e in enumerate((exx, ezz, eyy)):
            put(st, 6 + i, x, z, at(st, 6 + i, x, z) + (shear2 * e + bulk))
        for i, h in enumerate((hxz, hxy, hzy)):
            put(st, 9 + i, x, z, at(st, 9 + i, x, z) + shear * h)
        put(st, 12, x, z, at(st, 12, x, z) - bw)
        for i, e in enumerate((exx, ezz, eyy, hxz, hxy, hzy, w)):
            strain[i, x, pl.ds(z, chunk), :] = e

    def adj_at(f, x, z):
        return adj[f, x, pl.ds(z, chunk), :]

    def correlate(x, z, e, h, w, s, p, first_time):
        lame, shear, biot = [DT * mod(k, x, z) for k in range(3)]
        trace = s[0] + s[1] + s[2]
        dv = e[0] + e[1] + e[2]
        load = ALPHA * trace - p
        diag = s[0] * e[0] + s[1] * e[1] + s[2] * e[2]
        off = s[3] * h[0] + s[4] * h[1] + s[5] * h[2]
        for k, value in enumerate((trace * dv, 2.0 * diag + off, load * w)):
            value = DT * value
            if not first_time:
                value = grad[k, x, pl.ds(z, chunk), :] + value
            grad[k, x, pl.ds(z, chunk), :] = value
        t = biot * load
        bulk = lame * trace + ALPHA * t
        shear2 = 2.0 * shear
        for i in range(3):
            put(eh, i, x, z, shear2 * s[i] + bulk)
        for i in range(3):
            put(eh, 3 + i, x, z, shear * s[3 + i])
        put(eh, 6, x, z, t)

    def stress_back_2(x, z):
        exx, ezz, eyy, hxz, hxy, hzy, dv, w = strains(x, z, q2)
        final_p = at(st, 12, x, z) - DT * mod(2, x, z) * w
        s = [adj_at(6 + i, x, z) for i in range(6)]
        p = adj_at(12, x, z) + (hits[0, x, pl.ds(z, chunk), :] * final_p - seen[0, x, pl.ds(z, chunk), :])
        adj[12, x, pl.ds(z, chunk), :] = p
        correlate(x, z, (exx, ezz, eyy), (hxz, hxy, hzy), w, s, p, True)

    def velocity_bars(x, z, v, q):
        ex, ez, ey, hxz, hxy, hzy, t = [at(eh, i, x, z) for i in range(7)]
        vx = v[0] - (fwd(eh, 0, x, z, 0, ex) + bwd(eh, 3, x, z, 1, hxz) + bwd(eh, 4, x, z, 2, hxy))
        vz = v[1] - (bwd(eh, 3, x, z, 0, hxz) + fwd(eh, 1, x, z, 1, ez) + bwd(eh, 5, x, z, 2, hzy))
        vy = v[2] - (bwd(eh, 4, x, z, 0, hxy) + bwd(eh, 5, x, z, 1, hzy) + fwd(eh, 2, x, z, 2, ey))
        qs = [q[d] - fwd(eh, 6, x, z, d, t) for d in range(3)]
        return (vx, vz, vy), qs

    def velocity_back_2(x, z):
        v, q = velocity_bars(
            x, z, [adj_at(d, x, z) for d in range(3)], [adj_at(3 + d, x, z) for d in range(3)]
        )
        damp = mod(3, x, z)
        total = zero
        for d in range(3):
            r = C3 * q[d] - C2 * v[d]
            put(fr, d, x, z, C1 * v[d] - C2 * q[d])
            put(fr, 3 + d, x, z, r)
            total = total + at(q1, d, x, z) * r
            adj[d, x, pl.ds(z, chunk), :] = v[d]
            adj[3 + d, x, pl.ds(z, chunk), :] = q[d] - damp * r
        grad[3, x, pl.ds(z, chunk), :] = total

    def stress_back_1(x, z):
        fx, fz, fy = [at(fr, i, x, z) for i in range(3)]
        s = [
            adj_at(6, x, z) - bwd(fr, 0, x, z, 0, fx),
            adj_at(7, x, z) - bwd(fr, 1, x, z, 1, fz),
            adj_at(8, x, z) - bwd(fr, 2, x, z, 2, fy),
            adj_at(9, x, z) - (fwd(fr, 0, x, z, 1, fx) + fwd(fr, 1, x, z, 0, fz)),
            adj_at(10, x, z) - (fwd(fr, 0, x, z, 2, fx) + fwd(fr, 2, x, z, 0, fy)),
            adj_at(11, x, z) - (fwd(fr, 1, x, z, 2, fz) + fwd(fr, 2, x, z, 1, fy)),
        ]
        p = adj_at(12, x, z) + (
            bwd(fr, 3, x, z, 0) + bwd(fr, 4, x, z, 1) + bwd(fr, 5, x, z, 2)
        )
        e = [strain[i, x, pl.ds(z, chunk), :] for i in range(7)]
        correlate(x, z, e[0:3], e[3:6], e[6], s, p, False)

    def velocity_back_1(x, z):
        v, q = velocity_bars(
            x, z, [adj_at(d, x, z) for d in range(3)], [adj_at(3 + d, x, z) for d in range(3)]
        )
        total = grad[3, x, pl.ds(z, chunk), :]
        for d in range(3):
            total = total + at(st, 3 + d, x, z) * (C3 * q[d] - C2 * v[d])
        grad[3, x, pl.ds(z, chunk), :] = -total

    over_cells(0, lambda x, z: velocities(x, z, st, 3, q1))
    over_cells(1, stresses)

    src_x, src_z, src_y = place(cell_ref[0], nz, ny)

    @pl.when((src_x >= spans[1][0]) & (src_x < spans[1][1]))
    def _():
        here = lax.broadcasted_iota(jnp.int32, (1, ny), 1) == src_y
        at_source = (12, src_x + 1, pl.ds(GUARD + src_z, 1), slice(None))
        st[at_source] += jnp.where(here, amp_ref[0], 0.0)

    over_cells(2, lambda x, z: velocities(x, z, q1, 0, q2))
    over_cells(3, stress_back_2)
    over_cells(4, velocity_back_2)
    over_cells(5, stress_back_1)
    over_cells(6, velocity_back_1)

    if summed:
        low, high = summed
        span = high - low
        keep, send = outs

        def split(x, carry):
            for k in range(4):
                at = pl.ds((k * span + x) * piece, piece)
                for i in range(far):
                    for j in range(2):
                        rel = 4 * i + 2 * j
                        keep[j, i, at, :] = grad[k, low + x, rows_of(rel), :]
                        send[j, i, at, :] = grad[k, low + x, rows_of(rel + 1), :]
            return carry

        lax.fori_loop(0, span, split, 0)


def march(scalars, fields, n, spans, gathered=None, pieces=(), summed=None):
    _, nx, nz, ny = fields[NAMES.index("adj")].shape
    outs = [pltpu.VMEM(f.shape, F32) for f in fields]
    if summed:
        part = (2, n // 4, 4 * (summed[1] - summed[0]) * (nz // n), ny)
        outs += [pltpu.VMEM(part, F32)] * 2
    lead = len(scalars) + len(pieces)
    work = sum(end - begin for begin, end in spans)
    result = pl.pallas_call(
        functools.partial(march_kernel, n=n, spans=spans, gathered=gathered, summed=summed),
        out_shape=tuple(outs),
        in_specs=[SMEM] * len(scalars) + [VMEM] * (len(pieces) + len(fields)),
        out_specs=(VMEM,) * len(outs),
        input_output_aliases={lead + i: i for i in range(len(fields))},
        compiler_params=PARAMS,
        cost_estimate=cost(work * nz * ny, 100),
        name="march",
    )(*scalars, *[in_vmem(x) for x in (*pieces, *fields)])
    return result[: len(fields)], result[len(fields) :]


def partner(x, bit, n):
    return lax.ppermute(x, "shot", [(i, i ^ bit) for i in range(n)])


def gather_pieces(own, n):
    line = [own, *[partner(own, b, n) for b in range(4, n, 4)]]
    stacked = jnp.stack(line)
    across = partner(stacked, 2, n)
    return (*line, partner(stacked, 1, n), across, partner(across, 1, n))


def scatter_sum(keep, send, n):
    kept = keep + partner(send, 1, n)
    kept = kept[0] + partner(kept[1], 2, n)
    total = kept[0]
    for i in range(1, n // 4):
        total = total + partner(kept[i], 4 * i, n)
    return total


PASSES = 7


def per_device(
    forward_state,
    adjoint_state,
    source_amp,
    source_cell,
    receiver_cells,
    recorded,
    material,
    cell_class,
    class_factors,
):
    n = lax.axis_size("shot")
    me = lax.axis_index("shot").reshape(1)
    _, nx, piece, ny = material.shape
    parts = 2
    cut = [nx * i // parts for i in range(parts + 1)]
    factor, *owns = own_model(me, class_factors, cell_class, material, parts)
    pieces = [gather_pieces(own, n) for own in owns]
    scalars = (me, source_cell, source_amp[0])
    fields = load_fields(
        source_cell, source_amp[0], receiver_cells, recorded, forward_state[0], adjoint_state[0]
    )

    done = [0] * PASSES

    def upto(limits):
        spans = tuple((d, max(d, min(nx, limit))) for d, limit in zip(done, limits))
        done[:] = [end for _, end in spans]
        return spans

    for i in range(parts - 1):
        spans = upto([cut[i + 1] - p for p in range(PASSES)])
        fields, _ = march(scalars, fields, n, spans, (cut[i], cut[i + 1]), pieces[i])
    totals = []
    for i in range(parts):
        spans = upto([cut[i + 1] + PASSES - 1 - p for p in range(PASSES)])
        new = ((cut[-2], nx), pieces[-1]) if i == 0 else (None, ())
        fields, split = march(scalars, fields, n, spans, *new, summed=(cut[i], cut[i + 1]))
        totals.append(scatter_sum(*split, n))
    total = jnp.concatenate([t.reshape(4, -1, piece, ny) for t in totals], axis=1)
    return total * factor / jnp.sqrt(jnp.float32(forward_state.shape[0] * n))


def solution(mesh):
    placed = (
        P(("groups", "shot"), None, None, None, None),
        P(("groups", "shot"), None, None, None, None),
        P(("groups", "shot"), None),
        P(("groups", "shot")),
        P(("groups", "shot"), None),
        P(("groups", "shot"), None),
        P(None, "groups", "shot", None),
        P("groups", None, None),
        P(),
    )
    return jax.shard_map(
        per_device,
        mesh=mesh,
        in_specs=placed,
        out_specs=P(None, "groups", "shot", None),
        check_vma=False,
    )
```

```python
import functools

import jax
import jax.numpy as jnp
from jax import lax
from jax.experimental import pallas as pl
from jax.experimental.pallas import tpu as pltpu
from jax.sharding import PartitionSpec as P

ALPHA = 0.8
RHO_BULK = 2.2
RHO_FLUID = 1.0
MASS_FLUID = 2.5
DT = 0.25
DET = RHO_BULK * MASS_FLUID - RHO_FLUID * RHO_FLUID
C1 = DT * MASS_FLUID / DET
C2 = DT * RHO_FLUID / DET
C3 = DT * RHO_BULK / DET

GUARD = 8
CHUNK = 16
F32 = jnp.float32
BF16 = jnp.bfloat16
PARAMS = pltpu.CompilerParams(vmem_limit_bytes=12 * 1024 * 1024)
SMEM = pl.BlockSpec(memory_space=pltpu.SMEM)
VMEM = pl.BlockSpec(memory_space=pltpu.VMEM)
HBM = pl.BlockSpec(memory_space=pltpu.HBM)

RESIDENT = (
    ("st", 13, True),
    ("q1", 3, True),
    ("q2", 3, True),
    ("eh", 7, True),
    ("fr", 6, True),
    ("adj", 13, False),
    ("hits", 1, False),
    ("seen", 1, False),
    ("strain", 7, False),
    ("model", 4, False),
    ("grad", 4, False),
    ("source", 1, False),
)
NAMES = tuple(name for name, _, _ in RESIDENT)


def in_vmem(x):
    return pltpu.with_memory_space_constraint(x, pltpu.VMEM)


def in_hbm(x):
    return pltpu.with_memory_space_constraint(x, pltpu.HBM)


def cost(cells, ops):
    return pl.CostEstimate(flops=cells * ops, bytes_accessed=cells * 4, transcendentals=0)


def own_kernel(me_ref, class_factors, classes_hbm, material_hbm, factor, *refs):
    *owns, table_ref, classes, material, sems = refs
    _, nx, piece, ny = material.shape
    nx_part = nx // len(owns)
    rows = pl.ds(pl.multiple_of(me_ref[0] * piece, piece), piece)
    table_copy = pltpu.make_async_copy(class_factors, table_ref, sems.at[0])
    class_copy = pltpu.make_async_copy(classes_hbm, classes, sems.at[1])
    material_copy = pltpu.make_async_copy(material_hbm, material, sems.at[2])
    class_copy.start()
    material_copy.start()
    table_copy.start()
    table_copy.wait()
    class_copy.wait()
    material_copy.wait()
    table = [[table_ref[k, c] for c in range(class_factors.shape[1])] for k in range(4)]
    for x in range(nx):
        which = classes[x, rows, :]
        for k in range(4):
            f = jnp.full((piece, ny), table[k][0], F32)
            for c in range(1, len(table[k])):
                f = jnp.where(which == c, table[k][c], f)
            at = (k * nx_part + x % nx_part) * piece
            factor[k, x] = f
            owns[x // nx_part][0, at : at + piece, :] = f * material[k, x]


def own_model(me, class_factors, classes, material, parts):
    _, nx, piece, ny = material.shape
    part = (1, 4 * (nx // parts) * piece, ny)
    return pl.pallas_call(
        own_kernel,
        out_shape=(pltpu.VMEM(material.shape, F32), *[pltpu.VMEM(part, F32)] * parts),
        in_specs=[SMEM, HBM, HBM, HBM],
        out_specs=(VMEM,) * (parts + 1),
        scratch_shapes=[
            pltpu.SMEM(class_factors.shape, F32),
            pltpu.VMEM(classes.shape, jnp.int32),
            pltpu.VMEM(material.shape, F32),
            pltpu.SemaphoreType.DMA((3,)),
        ],
        compiler_params=PARAMS,
        cost_estimate=cost(4 * nx * piece * ny, 10),
        name="own_model",
    )(me, in_hbm(class_factors), in_hbm(classes), in_hbm(material))


def load_kernel(src_cell, amp_hbm, rec_cell_hbm, rec_hbm, state_hbm, adj_hbm, *refs, waits):
    refs = refs[waits:]
    amp_ref, cell_ref, rec_ref, sem_state, sem_adj, sem_small = refs[len(RESIDENT) :]
    r = dict(zip(NAMES, refs))
    nf, nx, nz, ny = state_hbm.shape
    st, adj, hits, seen = r["st"], r["adj"], r["hits"], r["seen"]
    copies = [
        pltpu.make_async_copy(
            state_hbm.at[f], st.at[f, pl.ds(1, nx), pl.ds(GUARD, nz), :], sem_state.at[f]
        )
        for f in range(nf)
    ]
    copies.append(pltpu.make_async_copy(adj_hbm, adj, sem_adj))
    small = [
        pltpu.make_async_copy(src, dst, sem_small.at[i])
        for i, (src, dst) in enumerate(
            ((rec_cell_hbm, cell_ref), (rec_hbm, rec_ref), (amp_hbm, amp_ref))
        )
    ]
    for copy in (*small, *copies):
        copy.start()

    zrow = jnp.zeros((GUARD, ny), F32)
    padded = [(r[name], f) for name, count, pad in RESIDENT if pad for f in range(count)]

    def zero_rows(x, carry):
        for ref, f in padded:
            ref[f, x, 0:GUARD, :] = zrow
            ref[f, x, nz + GUARD : nz + 2 * GUARD, :] = zrow
        return carry

    lax.fori_loop(0, nx + 2, zero_rows, 0)
    for ref, f in padded:
        for x in (0, nx + 1):
            for z in range(GUARD, nz + GUARD, GUARD):
                ref[f, x, z : z + GUARD, :] = zrow

    def zero_source(x, carry):
        r["source"][0, x] = jnp.zeros((nz, ny), F32)
        return carry

    lax.fori_loop(0, nx, zero_source, 0)
    for copy in small:
        copy.wait()

    cell, rec = cell_ref[...], rec_ref[...]
    count = cell.shape[1]
    row = lax.div(cell, ny)
    lane = cell - row * ny
    high = rec.astype(BF16).astype(F32)
    middle = (rec - high).astype(BF16).astype(F32)
    low = rec - high - middle
    match = lax.broadcasted_iota(jnp.int32, (ny, count), 0) == lane
    columns = jnp.concatenate(
        [jnp.where(match, v, 0.0).astype(BF16) for v in (jnp.ones_like(rec), high, middle, low)], 0
    )
    block = 128
    for b in range(0, nx * nz, block):
        rows = lax.broadcasted_iota(jnp.int32, (block, count), 0) + b == row
        out = lax.dot_general(
            jnp.where(rows, 1.0, 0.0).astype(BF16),
            columns,
            (((1,), (1,)), ((), ())),
            preferred_element_type=F32,
        )
        total = out[:, ny : 2 * ny] + out[:, 2 * ny : 3 * ny] + out[:, 3 * ny :]
        for z in range(0, block, nz):
            x = (b + z) // nz
            hits[0, x] = out[z : z + nz, :ny]
            seen[0, x] = total[z : z + nz]

    for copy in copies:
        copy.wait()

    src_x, src_z, src_y = place(src_cell[0], nz, ny)
    here = lax.broadcasted_iota(jnp.int32, (1, ny), 1) == src_y
    at = (src_x, pl.ds(src_z, 1), slice(None))
    r["source"][(0, *at)] = jnp.where(here, amp_ref[0, 0], 0.0)
    adj[(12, *at)] += jnp.where(here, hits[(0, *at)] * amp_ref[0, 1], 0.0)


def place(cell, nz, ny):
    return cell // (nz * ny), (cell // ny) % nz, cell % ny


def load_fields(cell, amps, receivers, recorded, state, adjoint, after):
    nf, nx, nz, ny = state.shape
    shapes = tuple(
        pltpu.VMEM((count, *((nx + 2, nz + 2 * GUARD, ny) if pad else (nx, nz, ny))), F32)
        for _, count, pad in RESIDENT
    )
    return pl.pallas_call(
        functools.partial(load_kernel, waits=len(after)),
        out_shape=shapes,
        in_specs=[SMEM] + [HBM] * 5 + [VMEM] * len(after),
        out_specs=(VMEM,) * len(shapes),
        scratch_shapes=[
            pltpu.SMEM(amps.shape, F32),
            pltpu.VMEM(receivers.shape, jnp.int32),
            pltpu.VMEM(recorded.shape, F32),
            pltpu.SemaphoreType.DMA((nf,)),
            pltpu.SemaphoreType.DMA,
            pltpu.SemaphoreType.DMA((3,)),
        ],
        compiler_params=PARAMS,
        cost_estimate=cost(nx * nz * ny, 150),
        name="load_fields",
    )(
        cell,
        *[in_hbm(x) for x in (amps, receivers, recorded, state, adjoint)],
        *[in_vmem(x) for x in after],
    )


def march_kernel(me_ref, *refs, n, spans, gathered, summed, waits):
    pieces = refs[: 2 * len(gathered)]
    refs = refs[len(pieces) + waits + len(RESIDENT) :]
    r = dict(zip(NAMES, refs))
    outs = refs[len(RESIDENT) :]
    st, q1, q2, eh, fr, adj, hits, seen, strain, model, grad, source = [r[name] for name in NAMES]
    _, nx, nz, ny = adj.shape
    piece = nz // n
    me = me_ref[0]

    def rows_of(rel):
        return pl.ds(pl.multiple_of((me ^ rel) * piece, piece), piece)

    for part, (low, high, rels) in enumerate(gathered):
        span = high - low
        near, core = pieces[2 * part : 2 * part + 2]

        def assemble(x, carry):
            for k in range(4):
                at = pl.ds((k * span + x) * piece, piece)
                for i, rel in enumerate(rels):
                    model[k, low + x, rows_of(rel), :] = near[i, at, :]
                    model[k, low + x, rows_of(rel ^ 1), :] = core[i, at, :]
            return carry

        lax.fori_loop(0, span, assemble, 0)

    lane = lax.broadcasted_iota(jnp.int32, (CHUNK, ny), 1)
    first, last = lane == 0, lane == ny - 1
    zero = jnp.zeros((CHUNK, ny), F32)
    chunk = CHUNK

    def at(ref, f, x, z, dx=0, dz=0):
        return ref[f, x + 1 + dx, pl.ds(GUARD + z + dz, chunk), :]

    def put(ref, f, x, z, value):
        ref[f, x + 1, pl.ds(GUARD + z, chunk), :] = value

    def ahead(f):
        return jnp.where(last, zero, pltpu.roll(f, ny - 1, 1))

    def behind(f):
        return jnp.where(first, zero, pltpu.roll(f, 1, 1))

    def fwd(ref, f, x, z, axis, here=None):
        here = at(ref, f, x, z) if here is None else here
        if axis == 0:
            return at(ref, f, x, z, dx=1) - here
        if axis == 1:
            return at(ref, f, x, z, dz=1) - here
        return ahead(here) - here

    def bwd(ref, f, x, z, axis, here=None):
        here = at(ref, f, x, z) if here is None else here
        if axis == 0:
            return here - at(ref, f, x, z, dx=-1)
        if axis == 1:
            return here - at(ref, f, x, z, dz=-1)
        return here - behind(here)

    def over_cells(number, body):
        begin, end = spans[number]

        def plane(x, carry):
            for z in range(0, nz, chunk):
                body(x, z)
            return carry

        if end > begin:
            lax.fori_loop(begin, end, plane, 0)

    def mod(k, x, z):
        return model[k, x, pl.ds(z, chunk), :]

    def forces(x, z):
        sxx, szz, syy, sxz, sxy, szy, p = [at(st, 6 + i, x, z) for i in range(7)]
        fx = fwd(st, 6, x, z, 0, sxx) + bwd(st, 9, x, z, 1, sxz) + bwd(st, 10, x, z, 2, sxy)
        fz = bwd(st, 9, x, z, 0, sxz) + fwd(st, 7, x, z, 1, szz) + bwd(st, 11, x, z, 2, szy)
        fy = bwd(st, 10, x, z, 0, sxy) + bwd(st, 11, x, z, 1, szy) + fwd(st, 8, x, z, 2, syy)
        g = [fwd(st, 12, x, z, d, p) for d in range(3)]
        return (fx, fz, fy), g

    def velocities(x, z, q_from, q_at, q_to):
        f, g = forces(x, z)
        damp = mod(3, x, z)
        for d in range(3):
            q = at(q_from, q_at + d, x, z)
            drag = g[d] + damp * q
            put(st, d, x, z, at(st, d, x, z) + (C1 * f[d] + C2 * drag))
            put(q_to, d, x, z, q - (C3 * drag + C2 * f[d]))

    def strains(x, z, q):
        vx, vz, vy = [at(st, i, x, z) for i in range(3)]
        exx = bwd(st, 0, x, z, 0, vx)
        ezz = bwd(st, 1, x, z, 1, vz)
        eyy = bwd(st, 2, x, z, 2, vy)
        dq = bwd(q, 0, x, z, 0) + bwd(q, 1, x, z, 1) + bwd(q, 2, x, z, 2)
        hxz = fwd(st, 0, x, z, 1, vx) + fwd(st, 1, x, z, 0, vz)
        hxy = fwd(st, 0, x, z, 2, vx) + fwd(st, 2, x, z, 0, vy)
        hzy = fwd(st, 1, x, z, 2, vz) + fwd(st, 2, x, z, 1, vy)
        dv = exx + ezz + eyy
        w = ALPHA * dv + dq
        return exx, ezz, eyy, hxz, hxy, hzy, dv, w

    def stresses(x, z):
        exx, ezz, eyy, hxz, hxy, hzy, dv, w = strains(x, z, q1)
        lame, shear, biot = [DT * mod(k, x, z) for k in range(3)]
        bw = biot * w
        bulk = lame * dv + ALPHA * bw
        shear2 = 2.0 * shear
        for i, e in enumerate((exx, ezz, eyy)):
            put(st, 6 + i, x, z, at(st, 6 + i, x, z) + (shear2 * e + bulk))
        for i, h in enumerate((hxz, hxy, hzy)):
            put(st, 9 + i, x, z, at(st, 9 + i, x, z) + shear * h)
        put(st, 12, x, z, at(st, 12, x, z) - bw + source[0, x, pl.ds(z, chunk), :])
        for i, e in enumerate((exx, ezz, eyy, hxz, hxy, hzy, w)):
            strain[i, x, pl.ds(z, chunk), :] = e

    def adj_at(f, x, z):
        return adj[f, x, pl.ds(z, chunk), :]

    def correlate(x, z, e, h, w, s, p, first_time):
        lame, shear, biot = [DT * mod(k, x, z) for k in range(3)]
        trace = s[0] + s[1] + s[2]
        dv = e[0] + e[1] + e[2]
        load = ALPHA * trace - p
        diag = s[0] * e[0] + s[1] * e[1] + s[2] * e[2]
        off = s[3] * h[0] + s[4] * h[1] + s[5] * h[2]
        for k, value in enumerate((trace * dv, 2.0 * diag + off, load * w)):
            value = DT * value
            if not first_time:
                value = grad[k, x, pl.ds(z, chunk), :] + value
            grad[k, x, pl.ds(z, chunk), :] = value
        t = biot * load
        bulk = lame * trace + ALPHA * t
        shear2 = 2.0 * shear
        for i in range(3):
            put(eh, i, x, z, shear2 * s[i] + bulk)
        for i in range(3):
            put(eh, 3 + i, x, z, shear * s[3 + i])
        put(eh, 6, x, z, t)

    def stress_back_2(x, z):
        exx, ezz, eyy, hxz, hxy, hzy, dv, w = strains(x, z, q2)
        final_p = at(st, 12, x, z) - DT * mod(2, x, z) * w
        s = [adj_at(6 + i, x, z) for i in range(6)]
        p = adj_at(12, x, z) + (hits[0, x, pl.ds(z, chunk), :] * final_p - seen[0, x, pl.ds(z, chunk), :])
        adj[12, x, pl.ds(z, chunk), :] = p
        correlate(x, z, (exx, ezz, eyy), (hxz, hxy, hzy), w, s, p, True)

    def velocity_bars(x, z, v, q):
        ex, ez, ey, hxz, hxy, hzy, t = [at(eh, i, x, z) for i in range(7)]
        vx = v[0] - (fwd(eh, 0, x, z, 0, ex) + bwd(eh, 3, x, z, 1, hxz) + bwd(eh, 4, x, z, 2, hxy))
        vz = v[1] - (bwd(eh, 3, x, z, 0, hxz) + fwd(eh, 1, x, z, 1, ez) + bwd(eh, 5, x, z, 2, hzy))
        vy = v[2] - (bwd(eh, 4, x, z, 0, hxy) + bwd(eh, 5, x, z, 1, hzy) + fwd(eh, 2, x, z, 2, ey))
        qs = [q[d] - fwd(eh, 6, x, z, d, t) for d in range(3)]
        return (vx, vz, vy), qs

    def velocity_back_2(x, z):
        v, q = velocity_bars(
            x, z, [adj_at(d, x, z) for d in range(3)], [adj_at(3 + d, x, z) for d in range(3)]
        )
        damp = mod(3, x, z)
        total = zero
        for d in range(3):
            r = C3 * q[d] - C2 * v[d]
            put(fr, d, x, z, C1 * v[d] - C2 * q[d])
            put(fr, 3 + d, x, z, r)
            total = total + at(q1, d, x, z) * r
            adj[d, x, pl.ds(z, chunk), :] = v[d]
            adj[3 + d, x, pl.ds(z, chunk), :] = q[d] - damp * r
        grad[3, x, pl.ds(z, chunk), :] = total

    def stress_back_1(x, z):
        fx, fz, fy = [at(fr, i, x, z) for i in range(3)]
        s = [
            adj_at(6, x, z) - bwd(fr, 0, x, z, 0, fx),
            adj_at(7, x, z) - bwd(fr, 1, x, z, 1, fz),
            adj_at(8, x, z) - bwd(fr, 2, x, z, 2, fy),
            adj_at(9, x, z) - (fwd(fr, 0, x, z, 1, fx) + fwd(fr, 1, x, z, 0, fz)),
            adj_at(10, x, z) - (fwd(fr, 0, x, z, 2, fx) + fwd(fr, 2, x, z, 0, fy)),
            adj_at(11, x, z) - (fwd(fr, 1, x, z, 2, fz) + fwd(fr, 2, x, z, 1, fy)),
        ]
        p = adj_at(12, x, z) + (
            bwd(fr, 3, x, z, 0) + bwd(fr, 4, x, z, 1) + bwd(fr, 5, x, z, 2)
        )
        e = [strain[i, x, pl.ds(z, chunk), :] for i in range(7)]
        correlate(x, z, e[0:3], e[3:6], e[6], s, p, False)

    def velocity_back_1(x, z):
        v, q = velocity_bars(
            x, z, [adj_at(d, x, z) for d in range(3)], [adj_at(3 + d, x, z) for d in range(3)]
        )
        total = grad[3, x, pl.ds(z, chunk), :]
        for d in range(3):
            total = total + at(st, 3 + d, x, z) * (C3 * q[d] - C2 * v[d])
        grad[3, x, pl.ds(z, chunk), :] = -total

    over_cells(0, lambda x, z: velocities(x, z, st, 3, q1))
    over_cells(1, stresses)

    over_cells(2, lambda x, z: velocities(x, z, q1, 0, q2))
    over_cells(3, stress_back_2)
    over_cells(4, velocity_back_2)
    over_cells(5, stress_back_1)
    over_cells(6, velocity_back_1)

    if summed:
        low, high, rels = summed
        span = high - low
        keep, send = outs

        def split(x, carry):
            for k in range(4):
                at = pl.ds((k * span + x) * piece, piece)
                for i, rel in enumerate(rels):
                    keep[i, at, :] = grad[k, low + x, rows_of(rel), :]
                    send[i, at, :] = grad[k, low + x, rows_of(rel ^ 1), :]
            return carry

        lax.fori_loop(0, span, split, 0)


def march(me, fields, n, spans, gathered=(), pieces=(), summed=None, after=()):
    _, nx, nz, ny = fields[NAMES.index("adj")].shape
    outs = [pltpu.VMEM(f.shape, F32) for f in fields]
    if summed:
        part = (n // 2, 4 * (summed[1] - summed[0]) * (nz // n), ny)
        outs += [pltpu.VMEM(part, F32)] * 2
    lead = 1 + len(pieces) + len(after)
    work = sum(end - begin for begin, end in spans)
    result = pl.pallas_call(
        functools.partial(
            march_kernel, n=n, spans=spans, gathered=gathered, summed=summed, waits=len(after)
        ),
        out_shape=tuple(outs),
        in_specs=[SMEM] + [VMEM] * (len(pieces) + len(after) + len(fields)),
        out_specs=(VMEM,) * len(outs),
        input_output_aliases={lead + i: i for i in range(len(fields))},
        compiler_params=PARAMS,
        cost_estimate=cost(work * nz * ny, 100),
        name="march",
    )(me, *[in_vmem(x) for x in (*pieces, *after, *fields)])
    return result[: len(fields)], result[len(fields) :]


def join(a, b, after=()):
    def kernel(a_ref, b_ref, *refs):
        out = refs[-1]
        out[: a.shape[0]] = a_ref[...]
        out[a.shape[0] :] = b_ref[...]

    return pl.pallas_call(
        kernel,
        out_shape=pltpu.VMEM((a.shape[0] + b.shape[0], *a.shape[1:]), F32),
        in_specs=[VMEM] * (2 + len(after)),
        out_specs=VMEM,
        compiler_params=PARAMS,
        cost_estimate=cost(2 * a.size, 1),
        name="join",
    )(*[in_vmem(x) for x in (a, b, *after)])


def add_halves(keep, came):
    half = keep.shape[0] // 2

    def kernel(a, b, low, high):
        low[...] = a[:half] + b[:half]
        high[...] = a[half:] + b[half:]

    return pl.pallas_call(
        kernel,
        out_shape=(pltpu.VMEM((half, *keep.shape[1:]), F32),) * 2,
        in_specs=[VMEM] * 2,
        out_specs=(VMEM,) * 2,
        compiler_params=PARAMS,
        cost_estimate=cost(keep.size, 1),
        name="add_halves",
    )(in_vmem(keep), in_vmem(came))


def finish(terms, cuts, factor, shape, scale):
    _, nx, piece, ny = shape

    def kernel(*refs):
        factor_ref, out = refs[-2:]
        for part, (low, high) in enumerate(zip(cuts, cuts[1:])):
            for x in range(low, high):
                for k in range(4):
                    at = (k * (high - low) + x - low) * piece
                    at = slice(at, at + piece)
                    total = refs[2 * part][0, at, :] + refs[2 * part + 1][0, at, :]
                    out[k, x] = total * factor_ref[k, x] * scale

    flat = [in_vmem(t) for part in terms for t in part]
    return pl.pallas_call(
        kernel,
        out_shape=jax.ShapeDtypeStruct(shape, F32),
        in_specs=[VMEM] * (len(flat) + 1),
        out_specs=VMEM,
        compiler_params=PARAMS,
        name="finish",
    )(*flat, in_vmem(factor))


def partner(x, bit, n):
    return lax.ppermute(x, "shot", [(i, i ^ bit) for i in range(n)])


PASSES = 7


def per_device(
    forward_state,
    adjoint_state,
    source_amp,
    source_cell,
    receiver_cells,
    recorded,
    material,
    cell_class,
    class_factors,
):
    n = lax.axis_size("shot")
    me = lax.axis_index("shot").reshape(1)
    nx = material.shape[1]
    along_z = [b for b in (4, 8, 16, 32, 64, 128) if b < n]

    factor, *owns = own_model(me, class_factors, cell_class, material, 2)
    ways = ([*along_z[::-1], 2], [2, *along_z[::-1]])
    data, rels = list(owns), [[0], [0]]
    fields, token = None, ()
    for step in range(len(ways[0])):
        came = [partner(d, way[step], n) for d, way in zip(data, ways)]
        if step == len(ways[0]) - 1:
            fields = load_fields(
                source_cell,
                source_amp,
                receiver_cells,
                recorded,
                forward_state[0],
                adjoint_state[0],
                data,
            )
            token = (fields[NAMES.index("hits")],)
        data = [join(d, c, token) for d, c in zip(data, came)]
        rels = [[*r, *[i ^ way[step] for i in r]] for r, way in zip(rels, ways)]
    pieces = [p for d in data for p in (d, partner(d, 1, n))]
    gathered = [(0, nx // 2, rels[0]), (nx // 2, nx, rels[1])]

    back = [2, *along_z]
    rels = [0]
    for b in back[::-1]:
        rels = [*rels, *[i ^ b for i in rels]]
    cuts = [0, nx // 2, nx * 3 // 4, nx]
    done = [0] * PASSES
    terms, after = [], ()
    for low, high in zip(cuts, cuts[1:]):
        limits = [min(nx, high + PASSES - 1 - p) for p in range(PASSES)]
        spans = tuple((d, max(d, limit)) for d, limit in zip(done, limits))
        done = [end for _, end in spans]
        if after:
            half = PASSES // 2
            early = (*spans[:half], *[(begin, begin) for begin, _ in spans[half:]])
            spans = (*[(end, end) for _, end in spans[:half]], *spans[half:])
            fields, _ = march(me, fields, n, early)
        fields, (keep, send) = march(
            me, fields, n, spans, gathered, pieces, (low, high, rels), after
        )
        gathered, pieces = (), ()
        came = partner(send, 1, n)
        for b in back:
            keep, send = add_halves(keep, came)
            if b == back[0]:
                after = (keep,)
            came = partner(send, b, n)
        terms.append((keep, came))
    scale = 1.0 / float(forward_state.shape[0] * n) ** 0.5
    return finish(terms, cuts, factor, material.shape, scale)


def solution(mesh):
    placed = (
        P(("groups", "shot"), None, None, None, None),
        P(("groups", "shot"), None, None, None, None),
        P(("groups", "shot"), None),
        P(("groups", "shot")),
        P(("groups", "shot"), None),
        P(("groups", "shot"), None),
        P(None, "groups", "shot", None),
        P("groups", None, None),
        P(),
    )
    return jax.shard_map(
        per_device,
        mesh=mesh,
        in_specs=placed,
        out_specs=P(None, "groups", "shot", None),
        check_vma=False,
    )
```

```python
import functools

import jax
import jax.numpy as jnp
from jax import lax
from jax.experimental import pallas as pl
from jax.experimental.pallas import tpu as pltpu
from jax.sharding import PartitionSpec as P

ALPHA = 0.8
RHO_BULK = 2.2
RHO_FLUID = 1.0
MASS_FLUID = 2.5
DT = 0.25
DET = RHO_BULK * MASS_FLUID - RHO_FLUID * RHO_FLUID
C1 = DT * MASS_FLUID / DET
C2 = DT * RHO_FLUID / DET
C3 = DT * RHO_BULK / DET

GUARD = 8
CHUNK = 16
UNROLL = 8
F32 = jnp.float32
BF16 = jnp.bfloat16
PARAMS = pltpu.CompilerParams(vmem_limit_bytes=12 * 1024 * 1024)
SMEM = pl.BlockSpec(memory_space=pltpu.SMEM)
VMEM = pl.BlockSpec(memory_space=pltpu.VMEM)
HBM = pl.BlockSpec(memory_space=pltpu.HBM)

RESIDENT = (
    ("st", 13, True),
    ("q1", 3, True),
    ("q2", 3, True),
    ("eh", 7, True),
    ("fr", 6, True),
    ("adj", 13, False),
    ("hits", 1, False),
    ("seen", 1, False),
    ("strain", 7, False),
    ("model", 4, False),
    ("grad", 4, False),
    ("source", 1, False),
)
NAMES = tuple(name for name, _, _ in RESIDENT)


def in_vmem(x):
    return pltpu.with_memory_space_constraint(x, pltpu.VMEM)


def in_hbm(x):
    return pltpu.with_memory_space_constraint(x, pltpu.HBM)


def cost(cells, ops):
    return pl.CostEstimate(flops=cells * ops, bytes_accessed=cells * 4, transcendentals=0)


def own_kernel(me_ref, class_factors, classes_hbm, material_hbm, factor, *refs):
    *owns, table_ref, classes, material, sems = refs
    _, nx, piece, ny = material.shape
    nx_part = nx // len(owns)
    rows = pl.ds(pl.multiple_of(me_ref[0] * piece, piece), piece)
    table_copy = pltpu.make_async_copy(class_factors, table_ref, sems.at[0])
    class_copy = pltpu.make_async_copy(classes_hbm, classes, sems.at[1])
    material_copy = pltpu.make_async_copy(material_hbm, material, sems.at[2])
    class_copy.start()
    material_copy.start()
    table_copy.start()
    table_copy.wait()
    class_copy.wait()
    material_copy.wait()
    table = [[table_ref[k, c] for c in range(class_factors.shape[1])] for k in range(4)]
    for x in range(nx):
        which = classes[x, rows, :]
        for k in range(4):
            f = jnp.full((piece, ny), table[k][0], F32)
            for c in range(1, len(table[k])):
                f = jnp.where(which == c, table[k][c], f)
            at = (k * nx_part + x % nx_part) * piece
            factor[k, x] = f
            owns[x // nx_part][0, at : at + piece, :] = f * material[k, x]


def own_model(me, class_factors, classes, material, parts):
    _, nx, piece, ny = material.shape
    part = (1, 4 * (nx // parts) * piece, ny)
    return pl.pallas_call(
        own_kernel,
        out_shape=(pltpu.VMEM(material.shape, F32), *[pltpu.VMEM(part, F32)] * parts),
        in_specs=[SMEM, HBM, HBM, HBM],
        out_specs=(VMEM,) * (parts + 1),
        scratch_shapes=[
            pltpu.SMEM(class_factors.shape, F32),
            pltpu.VMEM(classes.shape, jnp.int32),
            pltpu.VMEM(material.shape, F32),
            pltpu.SemaphoreType.DMA((3,)),
        ],
        compiler_params=PARAMS,
        cost_estimate=cost(4 * nx * piece * ny, 10),
        name="own_model",
    )(me, in_hbm(class_factors), in_hbm(classes), in_hbm(material))


def load_kernel(src_cell, amp_hbm, rec_cell_hbm, rec_hbm, state_hbm, adj_hbm, *refs, waits):
    refs = refs[waits:]
    amp_ref, cell_ref, rec_ref, sem_state, sem_adj, sem_small = refs[len(RESIDENT) :]
    r = dict(zip(NAMES, refs))
    nf, nx, nz, ny = state_hbm.shape
    st, adj, hits, seen = r["st"], r["adj"], r["hits"], r["seen"]
    copies = [
        pltpu.make_async_copy(
            state_hbm.at[f], st.at[f, pl.ds(1, nx), pl.ds(GUARD, nz), :], sem_state.at[f]
        )
        for f in range(nf)
    ]
    copies.append(pltpu.make_async_copy(adj_hbm, adj, sem_adj))
    small = [
        pltpu.make_async_copy(src, dst, sem_small.at[i])
        for i, (src, dst) in enumerate(
            ((rec_cell_hbm, cell_ref), (rec_hbm, rec_ref), (amp_hbm, amp_ref))
        )
    ]
    for copy in (*small, *copies):
        copy.start()

    zrow = jnp.zeros((GUARD, ny), F32)
    padded = [(r[name], f) for name, count, pad in RESIDENT if pad for f in range(count)]

    def zero_rows(x, carry):
        for ref, f in padded:
            ref[f, x, 0:GUARD, :] = zrow
            ref[f, x, nz + GUARD : nz + 2 * GUARD, :] = zrow
        return carry

    lax.fori_loop(0, nx + 2, zero_rows, 0)
    for ref, f in padded:
        for x in (0, nx + 1):
            for z in range(GUARD, nz + GUARD, GUARD):
                ref[f, x, z : z + GUARD, :] = zrow

    def zero_source(x, carry):
        r["source"][0, x] = jnp.zeros((nz, ny), F32)
        return carry

    lax.fori_loop(0, nx, zero_source, 0)
    for copy in small:
        copy.wait()

    cell, rec = cell_ref[...], rec_ref[...]
    count = cell.shape[1]
    row = lax.div(cell, ny)
    lane = cell - row * ny
    high = rec.astype(BF16).astype(F32)
    middle = (rec - high).astype(BF16).astype(F32)
    low = rec - high - middle
    match = lax.broadcasted_iota(jnp.int32, (ny, count), 0) == lane
    columns = jnp.concatenate(
        [jnp.where(match, v, 0.0).astype(BF16) for v in (jnp.ones_like(rec), high, middle, low)], 0
    )
    block = 128
    for b in range(0, nx * nz, block):
        rows = lax.broadcasted_iota(jnp.int32, (block, count), 0) + b == row
        out = lax.dot_general(
            jnp.where(rows, 1.0, 0.0).astype(BF16),
            columns,
            (((1,), (1,)), ((), ())),
            preferred_element_type=F32,
        )
        total = out[:, ny : 2 * ny] + out[:, 2 * ny : 3 * ny] + out[:, 3 * ny :]
        for z in range(0, block, nz):
            x = (b + z) // nz
            hits[0, x] = out[z : z + nz, :ny]
            seen[0, x] = total[z : z + nz]

    for copy in copies:
        copy.wait()

    src_x, src_z, src_y = place(src_cell[0], nz, ny)
    here = lax.broadcasted_iota(jnp.int32, (1, ny), 1) == src_y
    at = (src_x, pl.ds(src_z, 1), slice(None))
    r["source"][(0, *at)] = jnp.where(here, amp_ref[0, 0], 0.0)
    adj[(12, *at)] += jnp.where(here, hits[(0, *at)] * amp_ref[0, 1], 0.0)


def place(cell, nz, ny):
    return cell // (nz * ny), (cell // ny) % nz, cell % ny


def load_fields(cell, amps, receivers, recorded, state, adjoint, after):
    nf, nx, nz, ny = state.shape
    shapes = tuple(
        pltpu.VMEM((count, *((nx + 2, nz + 2 * GUARD, ny) if pad else (nx, nz, ny))), F32)
        for _, count, pad in RESIDENT
    )
    return pl.pallas_call(
        functools.partial(load_kernel, waits=len(after)),
        out_shape=shapes,
        in_specs=[SMEM] + [HBM] * 5 + [VMEM] * len(after),
        out_specs=(VMEM,) * len(shapes),
        scratch_shapes=[
            pltpu.SMEM(amps.shape, F32),
            pltpu.VMEM(receivers.shape, jnp.int32),
            pltpu.VMEM(recorded.shape, F32),
            pltpu.SemaphoreType.DMA((nf,)),
            pltpu.SemaphoreType.DMA,
            pltpu.SemaphoreType.DMA((3,)),
        ],
        compiler_params=PARAMS,
        cost_estimate=cost(nx * nz * ny, 150),
        name="load_fields",
    )(
        cell,
        *[in_hbm(x) for x in (amps, receivers, recorded, state, adjoint)],
        *[in_vmem(x) for x in after],
    )


def march_kernel(me_ref, *refs, n, spans, gathered, summed, waits):
    pieces = refs[: 2 * len(gathered)]
    refs = refs[len(pieces) + waits + len(RESIDENT) :]
    r = dict(zip(NAMES, refs))
    outs = refs[len(RESIDENT) :]
    st, q1, q2, eh, fr, adj, hits, seen, strain, model, grad, source = [r[name] for name in NAMES]
    _, nx, nz, ny = adj.shape
    piece = nz // n
    me = me_ref[0]

    def rows_of(rel):
        return pl.ds(pl.multiple_of((me ^ rel) * piece, piece), piece)

    for part, (low, high, rels) in enumerate(gathered):
        span = high - low
        near, core = pieces[2 * part : 2 * part + 2]

        def assemble(x, carry):
            for k in range(4):
                at = pl.ds((k * span + x) * piece, piece)
                for i, rel in enumerate(rels):
                    model[k, low + x, rows_of(rel), :] = near[i, at, :]
                    model[k, low + x, rows_of(rel ^ 1), :] = core[i, at, :]
            return carry

        lax.fori_loop(0, span, assemble, 0)

    lane = lax.broadcasted_iota(jnp.int32, (CHUNK, ny), 1)
    first, last = lane == 0, lane == ny - 1
    zero = jnp.zeros((CHUNK, ny), F32)
    chunk = CHUNK

    def at(ref, f, x, z, dx=0, dz=0):
        return ref[f, x + 1 + dx, pl.ds(GUARD + z + dz, chunk), :]

    def put(ref, f, x, z, value):
        ref[f, x + 1, pl.ds(GUARD + z, chunk), :] = value

    def ahead(f):
        return jnp.where(last, zero, pltpu.roll(f, ny - 1, 1))

    def behind(f):
        return jnp.where(first, zero, pltpu.roll(f, 1, 1))

    def fwd(ref, f, x, z, axis, here=None):
        here = at(ref, f, x, z) if here is None else here
        if axis == 0:
            return at(ref, f, x, z, dx=1) - here
        if axis == 1:
            return at(ref, f, x, z, dz=1) - here
        return ahead(here) - here

    def bwd(ref, f, x, z, axis, here=None):
        here = at(ref, f, x, z) if here is None else here
        if axis == 0:
            return here - at(ref, f, x, z, dx=-1)
        if axis == 1:
            return here - at(ref, f, x, z, dz=-1)
        return here - behind(here)

    def over_cells(number, body):
        begin, end = spans[number]

        def plane(x):
            for z in range(0, nz, chunk):
                body(x, z)

        def planes(i, carry):
            for x in range(UNROLL):
                plane(begin + i * UNROLL + x)
            return carry

        whole = (end - begin) // UNROLL
        if whole:
            lax.fori_loop(0, whole, planes, 0)
        for x in range(begin + whole * UNROLL, end):
            plane(x)

    def mod(k, x, z):
        return model[k, x, pl.ds(z, chunk), :]

    def forces(x, z):
        sxx, szz, syy, sxz, sxy, szy, p = [at(st, 6 + i, x, z) for i in range(7)]
        fx = fwd(st, 6, x, z, 0, sxx) + bwd(st, 9, x, z, 1, sxz) + bwd(st, 10, x, z, 2, sxy)
        fz = bwd(st, 9, x, z, 0, sxz) + fwd(st, 7, x, z, 1, szz) + bwd(st, 11, x, z, 2, szy)
        fy = bwd(st, 10, x, z, 0, sxy) + bwd(st, 11, x, z, 1, szy) + fwd(st, 8, x, z, 2, syy)
        g = [fwd(st, 12, x, z, d, p) for d in range(3)]
        return (fx, fz, fy), g

    def velocities(x, z, q_from, q_at, q_to):
        f, g = forces(x, z)
        damp = mod(3, x, z)
        for d in range(3):
            q = at(q_from, q_at + d, x, z)
            drag = g[d] + damp * q
            put(st, d, x, z, at(st, d, x, z) + (C1 * f[d] + C2 * drag))
            put(q_to, d, x, z, q - (C3 * drag + C2 * f[d]))

    def strains(x, z, q):
        vx, vz, vy = [at(st, i, x, z) for i in range(3)]
        exx = bwd(st, 0, x, z, 0, vx)
        ezz = bwd(st, 1, x, z, 1, vz)
        eyy = bwd(st, 2, x, z, 2, vy)
        dq = bwd(q, 0, x, z, 0) + bwd(q, 1, x, z, 1) + bwd(q, 2, x, z, 2)
        hxz = fwd(st, 0, x, z, 1, vx) + fwd(st, 1, x, z, 0, vz)
        hxy = fwd(st, 0, x, z, 2, vx) + fwd(st, 2, x, z, 0, vy)
        hzy = fwd(st, 1, x, z, 2, vz) + fwd(st, 2, x, z, 1, vy)
        dv = exx + ezz + eyy
        w = ALPHA * dv + dq
        return exx, ezz, eyy, hxz, hxy, hzy, dv, w

    def stresses(x, z):
        exx, ezz, eyy, hxz, hxy, hzy, dv, w = strains(x, z, q1)
        lame, shear, biot = [DT * mod(k, x, z) for k in range(3)]
        bw = biot * w
        bulk = lame * dv + ALPHA * bw
        shear2 = 2.0 * shear
        for i, e in enumerate((exx, ezz, eyy)):
            put(st, 6 + i, x, z, at(st, 6 + i, x, z) + (shear2 * e + bulk))
        for i, h in enumerate((hxz, hxy, hzy)):
            put(st, 9 + i, x, z, at(st, 9 + i, x, z) + shear * h)
        put(st, 12, x, z, at(st, 12, x, z) - bw + source[0, x, pl.ds(z, chunk), :])
        for i, e in enumerate((exx, ezz, eyy, hxz, hxy, hzy, w)):
            strain[i, x, pl.ds(z, chunk), :] = e

    def adj_at(f, x, z):
        return adj[f, x, pl.ds(z, chunk), :]

    def correlate(x, z, e, h, w, s, p, first_time):
        lame, shear, biot = [DT * mod(k, x, z) for k in range(3)]
        trace = s[0] + s[1] + s[2]
        dv = e[0] + e[1] + e[2]
        load = ALPHA * trace - p
        diag = s[0] * e[0] + s[1] * e[1] + s[2] * e[2]
        off = s[3] * h[0] + s[4] * h[1] + s[5] * h[2]
        for k, value in enumerate((trace * dv, 2.0 * diag + off, load * w)):
            value = DT * value
            if not first_time:
                value = grad[k, x, pl.ds(z, chunk), :] + value
            grad[k, x, pl.ds(z, chunk), :] = value
        t = biot * load
        bulk = lame * trace + ALPHA * t
        shear2 = 2.0 * shear
        for i in range(3):
            put(eh, i, x, z, shear2 * s[i] + bulk)
        for i in range(3):
            put(eh, 3 + i, x, z, shear * s[3 + i])
        put(eh, 6, x, z, t)

    def stress_back_2(x, z):
        exx, ezz, eyy, hxz, hxy, hzy, dv, w = strains(x, z, q2)
        final_p = at(st, 12, x, z) - DT * mod(2, x, z) * w
        s = [adj_at(6 + i, x, z) for i in range(6)]
        p = adj_at(12, x, z) + (hits[0, x, pl.ds(z, chunk), :] * final_p - seen[0, x, pl.ds(z, chunk), :])
        adj[12, x, pl.ds(z, chunk), :] = p
        correlate(x, z, (exx, ezz, eyy), (hxz, hxy, hzy), w, s, p, True)

    def velocity_bars(x, z, v, q):
        ex, ez, ey, hxz, hxy, hzy, t = [at(eh, i, x, z) for i in range(7)]
        vx = v[0] - (fwd(eh, 0, x, z, 0, ex) + bwd(eh, 3, x, z, 1, hxz) + bwd(eh, 4, x, z, 2, hxy))
        vz = v[1] - (bwd(eh, 3, x, z, 0, hxz) + fwd(eh, 1, x, z, 1, ez) + bwd(eh, 5, x, z, 2, hzy))
        vy = v[2] - (bwd(eh, 4, x, z, 0, hxy) + bwd(eh, 5, x, z, 1, hzy) + fwd(eh, 2, x, z, 2, ey))
        qs = [q[d] - fwd(eh, 6, x, z, d, t) for d in range(3)]
        return (vx, vz, vy), qs

    def velocity_back_2(x, z):
        v, q = velocity_bars(
            x, z, [adj_at(d, x, z) for d in range(3)], [adj_at(3 + d, x, z) for d in range(3)]
        )
        damp = mod(3, x, z)
        total = zero
        for d in range(3):
            r = C3 * q[d] - C2 * v[d]
            put(fr, d, x, z, C1 * v[d] - C2 * q[d])
            put(fr, 3 + d, x, z, r)
            total = total + at(q1, d, x, z) * r
            adj[d, x, pl.ds(z, chunk), :] = v[d]
            adj[3 + d, x, pl.ds(z, chunk), :] = q[d] - damp * r
        grad[3, x, pl.ds(z, chunk), :] = total

    def stress_back_1(x, z):
        fx, fz, fy = [at(fr, i, x, z) for i in range(3)]
        s = [
            adj_at(6, x, z) - bwd(fr, 0, x, z, 0, fx),
            adj_at(7, x, z) - bwd(fr, 1, x, z, 1, fz),
            adj_at(8, x, z) - bwd(fr, 2, x, z, 2, fy),
            adj_at(9, x, z) - (fwd(fr, 0, x, z, 1, fx) + fwd(fr, 1, x, z, 0, fz)),
            adj_at(10, x, z) - (fwd(fr, 0, x, z, 2, fx) + fwd(fr, 2, x, z, 0, fy)),
            adj_at(11, x, z) - (fwd(fr, 1, x, z, 2, fz) + fwd(fr, 2, x, z, 1, fy)),
        ]
        p = adj_at(12, x, z) + (
            bwd(fr, 3, x, z, 0) + bwd(fr, 4, x, z, 1) + bwd(fr, 5, x, z, 2)
        )
        e = [strain[i, x, pl.ds(z, chunk), :] for i in range(7)]
        correlate(x, z, e[0:3], e[3:6], e[6], s, p, False)

    def velocity_back_1(x, z):
        v, q = velocity_bars(
            x, z, [adj_at(d, x, z) for d in range(3)], [adj_at(3 + d, x, z) for d in range(3)]
        )
        total = grad[3, x, pl.ds(z, chunk), :]
        for d in range(3):
            total = total + at(st, 3 + d, x, z) * (C3 * q[d] - C2 * v[d])
        grad[3, x, pl.ds(z, chunk), :] = -total

    over_cells(0, lambda x, z: velocities(x, z, st, 3, q1))
    over_cells(1, stresses)

    over_cells(2, lambda x, z: velocities(x, z, q1, 0, q2))
    over_cells(3, stress_back_2)
    over_cells(4, velocity_back_2)
    over_cells(5, stress_back_1)
    over_cells(6, velocity_back_1)

    if summed:
        low, high, rels = summed
        span = high - low
        keep, send = outs

        def split(x, carry):
            for k in range(4):
                at = pl.ds((k * span + x) * piece, piece)
                for i, rel in enumerate(rels):
                    keep[i, at, :] = grad[k, low + x, rows_of(rel), :]
                    send[i, at, :] = grad[k, low + x, rows_of(rel ^ 1), :]
            return carry

        lax.fori_loop(0, span, split, 0)


def march(me, fields, n, spans, gathered=(), pieces=(), summed=None, after=()):
    _, nx, nz, ny = fields[NAMES.index("adj")].shape
    outs = [pltpu.VMEM(f.shape, F32) for f in fields]
    if summed:
        part = (n // 2, 4 * (summed[1] - summed[0]) * (nz // n), ny)
        outs += [pltpu.VMEM(part, F32)] * 2
    lead = 1 + len(pieces) + len(after)
    work = sum(end - begin for begin, end in spans)
    result = pl.pallas_call(
        functools.partial(
            march_kernel, n=n, spans=spans, gathered=gathered, summed=summed, waits=len(after)
        ),
        out_shape=tuple(outs),
        in_specs=[SMEM] + [VMEM] * (len(pieces) + len(after) + len(fields)),
        out_specs=(VMEM,) * len(outs),
        input_output_aliases={lead + i: i for i in range(len(fields))},
        compiler_params=PARAMS,
        cost_estimate=cost(work * nz * ny, 100),
        name="march",
    )(me, *[in_vmem(x) for x in (*pieces, *after, *fields)])
    return result[: len(fields)], result[len(fields) :]


def join(a, b, after=()):
    def kernel(a_ref, b_ref, *refs):
        out = refs[-1]
        out[: a.shape[0]] = a_ref[...]
        out[a.shape[0] :] = b_ref[...]

    return pl.pallas_call(
        kernel,
        out_shape=pltpu.VMEM((a.shape[0] + b.shape[0], *a.shape[1:]), F32),
        in_specs=[VMEM] * (2 + len(after)),
        out_specs=VMEM,
        compiler_params=PARAMS,
        cost_estimate=cost(2 * a.size, 1),
        name="join",
    )(*[in_vmem(x) for x in (a, b, *after)])


def add_halves(keep, came, after=()):
    half = keep.shape[0] // 2

    def kernel(a, b, *refs):
        low, high = refs[-2:]
        low[...] = a[:half] + b[:half]
        high[...] = a[half:] + b[half:]

    return pl.pallas_call(
        kernel,
        out_shape=(pltpu.VMEM((half, *keep.shape[1:]), F32),) * 2,
        in_specs=[VMEM] * (2 + len(after)),
        out_specs=(VMEM,) * 2,
        compiler_params=PARAMS,
        cost_estimate=cost(keep.size, 1),
        name="add_halves",
    )(*[in_vmem(x) for x in (keep, came, *after)])


def finish(terms, cuts, factor, shape, scale):
    _, nx, piece, ny = shape

    def kernel(*refs):
        factor_ref, out = refs[-2:]
        for part, (low, high) in enumerate(zip(cuts, cuts[1:])):
            for x in range(low, high):
                for k in range(4):
                    at = (k * (high - low) + x - low) * piece
                    at = slice(at, at + piece)
                    total = refs[2 * part][0, at, :] + refs[2 * part + 1][0, at, :]
                    out[k, x] = total * factor_ref[k, x] * scale

    flat = [in_vmem(t) for part in terms for t in part]
    return pl.pallas_call(
        kernel,
        out_shape=jax.ShapeDtypeStruct(shape, F32),
        in_specs=[VMEM] * (len(flat) + 1),
        out_specs=VMEM,
        compiler_params=PARAMS,
        name="finish",
    )(*flat, in_vmem(factor))


def partner(x, bit, n):
    return lax.ppermute(x, "shot", [(i, i ^ bit) for i in range(n)])


PASSES = 7


def per_device(
    forward_state,
    adjoint_state,
    source_amp,
    source_cell,
    receiver_cells,
    recorded,
    material,
    cell_class,
    class_factors,
):
    n = lax.axis_size("shot")
    me = lax.axis_index("shot").reshape(1)
    nx = material.shape[1]
    along_z = [b for b in (4, 8, 16, 32, 64, 128) if b < n]

    factor, *owns = own_model(me, class_factors, cell_class, material, 2)
    ways = ([*along_z[::-1], 2], [2, *along_z[::-1]])
    data, rels = list(owns), [[0], [0]]
    fields, token = None, ()
    for step in range(len(ways[0])):
        came = [partner(d, way[step], n) for d, way in zip(data, ways)]
        if step == len(ways[0]) - 1:
            fields = load_fields(
                source_cell,
                source_amp,
                receiver_cells,
                recorded,
                forward_state[0],
                adjoint_state[0],
                data,
            )
            token = (fields[NAMES.index("hits")],)
        data = [join(d, c, token) for d, c in zip(data, came)]
        rels = [[*r, *[i ^ way[step] for i in r]] for r, way in zip(rels, ways)]
    pieces = [p for d in data for p in (d, partner(d, 1, n))]
    gathered = [(0, nx // 2, rels[0]), (nx // 2, nx, rels[1])]

    backs = ([2, *along_z], [*along_z, 2])
    cuts = [0, nx * 5 // 8, nx]
    done = [0] * PASSES
    terms = []
    for low, high, back in zip(cuts, cuts[1:], backs):
        rels = [0]
        for b in back[::-1]:
            rels = [*rels, *[i ^ b for i in rels]]
        limits = [min(nx, high + PASSES - 1 - p) for p in range(PASSES)]
        spans = tuple((d, max(d, limit)) for d, limit in zip(done, limits))
        done = [end for _, end in spans]
        fields, (keep, send) = march(me, fields, n, spans, gathered, pieces, (low, high, rels))
        gathered, pieces = (), ()
        came = partner(send, 1, n)
        for b in back:
            keep, send = add_halves(keep, came)
            came = partner(send, b, n)
        terms.append((keep, came))
    scale = 1.0 / float(forward_state.shape[0] * n) ** 0.5
    return finish(terms, cuts, factor, material.shape, scale)


def solution(mesh):
    placed = (
        P(("groups", "shot"), None, None, None, None),
        P(("groups", "shot"), None, None, None, None),
        P(("groups", "shot"), None),
        P(("groups", "shot")),
        P(("groups", "shot"), None),
        P(("groups", "shot"), None),
        P(None, "groups", "shot", None),
        P("groups", None, None),
        P(),
    )
    return jax.shard_map(
        per_device,
        mesh=mesh,
        in_specs=placed,
        out_specs=P(None, "groups", "shot", None),
        check_vma=False,
    )
```

```python
import functools

import jax
import jax.numpy as jnp
from jax import lax
from jax.experimental import pallas as pl
from jax.experimental.pallas import tpu as pltpu
from jax.sharding import PartitionSpec as P

ALPHA = 0.8
RHO_BULK = 2.2
RHO_FLUID = 1.0
MASS_FLUID = 2.5
DT = 0.25
DET = RHO_BULK * MASS_FLUID - RHO_FLUID * RHO_FLUID
C1 = DT * MASS_FLUID / DET
C2 = DT * RHO_FLUID / DET
C3 = DT * RHO_BULK / DET

GUARD = 8
CHUNK = 16
UNROLL = 8
F32 = jnp.float32
BF16 = jnp.bfloat16
PARAMS = pltpu.CompilerParams(vmem_limit_bytes=12 * 1024 * 1024)
SMEM = pl.BlockSpec(memory_space=pltpu.SMEM)
VMEM = pl.BlockSpec(memory_space=pltpu.VMEM)
HBM = pl.BlockSpec(memory_space=pltpu.HBM)

RESIDENT = (
    ("st", 13, True),
    ("q1", 3, True),
    ("q2", 3, True),
    ("eh", 7, True),
    ("fr", 6, True),
    ("adj", 13, False),
    ("hits", 1, False),
    ("seen", 1, False),
    ("strain", 7, False),
    ("model", 4, False),
    ("grad", 4, False),
    ("source", 1, False),
)
NAMES = tuple(name for name, _, _ in RESIDENT)


def in_vmem(x):
    return pltpu.with_memory_space_constraint(x, pltpu.VMEM)


def in_hbm(x):
    return pltpu.with_memory_space_constraint(x, pltpu.HBM)


def cost(cells, ops):
    return pl.CostEstimate(flops=cells * ops, bytes_accessed=cells * 4, transcendentals=0)


def own_kernel(me_ref, class_factors, classes_hbm, material_hbm, factor, *refs):
    *owns, table_ref, classes, material, sems = refs
    _, nx, piece, ny = material.shape
    nx_part = nx // len(owns)
    rows = pl.ds(pl.multiple_of(me_ref[0] * piece, piece), piece)
    table_copy = pltpu.make_async_copy(class_factors, table_ref, sems.at[0])
    class_copy = pltpu.make_async_copy(classes_hbm, classes, sems.at[1])
    material_copy = pltpu.make_async_copy(material_hbm, material, sems.at[2])
    class_copy.start()
    material_copy.start()
    table_copy.start()
    table_copy.wait()
    class_copy.wait()
    material_copy.wait()
    table = [[table_ref[k, c] for c in range(class_factors.shape[1])] for k in range(4)]
    for x in range(nx):
        which = classes[x, rows, :]
        for k in range(4):
            f = jnp.full((piece, ny), table[k][0], F32)
            for c in range(1, len(table[k])):
                f = jnp.where(which == c, table[k][c], f)
            at = (k * nx_part + x % nx_part) * piece
            factor[k, x] = f
            owns[x // nx_part][0, at : at + piece, :] = f * material[k, x]


def own_model(me, class_factors, classes, material, parts):
    _, nx, piece, ny = material.shape
    part = (1, 4 * (nx // parts) * piece, ny)
    return pl.pallas_call(
        own_kernel,
        out_shape=(pltpu.VMEM(material.shape, F32), *[pltpu.VMEM(part, F32)] * parts),
        in_specs=[SMEM, HBM, HBM, HBM],
        out_specs=(VMEM,) * (parts + 1),
        scratch_shapes=[
            pltpu.SMEM(class_factors.shape, F32),
            pltpu.VMEM(classes.shape, jnp.int32),
            pltpu.VMEM(material.shape, F32),
            pltpu.SemaphoreType.DMA((3,)),
        ],
        compiler_params=PARAMS,
        cost_estimate=cost(4 * nx * piece * ny, 10),
        name="own_model",
    )(me, in_hbm(class_factors), in_hbm(classes), in_hbm(material))


def load_kernel(src_cell, amp_hbm, rec_cell_hbm, rec_hbm, state_hbm, adj_hbm, *refs, waits):
    refs = refs[waits:]
    amp_ref, cell_ref, rec_ref, sem_state, sem_adj, sem_small = refs[len(RESIDENT) :]
    r = dict(zip(NAMES, refs))
    nf, nx, nz, ny = state_hbm.shape
    st, adj, hits, seen = r["st"], r["adj"], r["hits"], r["seen"]
    copies = [
        pltpu.make_async_copy(
            state_hbm.at[f], st.at[f, pl.ds(1, nx), pl.ds(GUARD, nz), :], sem_state.at[f]
        )
        for f in range(nf)
    ]
    copies.append(pltpu.make_async_copy(adj_hbm, adj, sem_adj))
    small = [
        pltpu.make_async_copy(src, dst, sem_small.at[i])
        for i, (src, dst) in enumerate(
            ((rec_cell_hbm, cell_ref), (rec_hbm, rec_ref), (amp_hbm, amp_ref))
        )
    ]
    for copy in (*small, *copies):
        copy.start()

    zrow = jnp.zeros((GUARD, ny), F32)
    padded = [(r[name], f) for name, count, pad in RESIDENT if pad for f in range(count)]

    def zero_rows(x, carry):
        for ref, f in padded:
            ref[f, x, 0:GUARD, :] = zrow
            ref[f, x, nz + GUARD : nz + 2 * GUARD, :] = zrow
        return carry

    lax.fori_loop(0, nx + 2, zero_rows, 0)
    for ref, f in padded:
        for x in (0, nx + 1):
            for z in range(GUARD, nz + GUARD, GUARD):
                ref[f, x, z : z + GUARD, :] = zrow

    def zero_source(x, carry):
        r["source"][0, x] = jnp.zeros((nz, ny), F32)
        return carry

    lax.fori_loop(0, nx, zero_source, 0)
    for copy in small:
        copy.wait()

    cell, rec = cell_ref[...], rec_ref[...]
    count = cell.shape[1]
    row = lax.div(cell, ny)
    lane = cell - row * ny
    high = rec.astype(BF16).astype(F32)
    middle = (rec - high).astype(BF16).astype(F32)
    low = rec - high - middle
    match = lax.broadcasted_iota(jnp.int32, (ny, count), 0) == lane
    columns = jnp.concatenate(
        [jnp.where(match, v, 0.0).astype(BF16) for v in (jnp.ones_like(rec), high, middle, low)], 0
    )
    block = 128
    for b in range(0, nx * nz, block):
        rows = lax.broadcasted_iota(jnp.int32, (block, count), 0) + b == row
        out = lax.dot_general(
            jnp.where(rows, 1.0, 0.0).astype(BF16),
            columns,
            (((1,), (1,)), ((), ())),
            preferred_element_type=F32,
        )
        total = out[:, ny : 2 * ny] + out[:, 2 * ny : 3 * ny] + out[:, 3 * ny :]
        for z in range(0, block, nz):
            x = (b + z) // nz
            hits[0, x] = out[z : z + nz, :ny]
            seen[0, x] = total[z : z + nz]

    for copy in copies:
        copy.wait()

    src_x, src_z, src_y = place(src_cell[0], nz, ny)
    here = lax.broadcasted_iota(jnp.int32, (1, ny), 1) == src_y
    at = (src_x, pl.ds(src_z, 1), slice(None))
    r["source"][(0, *at)] = jnp.where(here, amp_ref[0, 0], 0.0)
    adj[(12, *at)] += jnp.where(here, hits[(0, *at)] * amp_ref[0, 1], 0.0)


def place(cell, nz, ny):
    return cell // (nz * ny), (cell // ny) % nz, cell % ny


def load_fields(cell, amps, receivers, recorded, state, adjoint, after):
    nf, nx, nz, ny = state.shape
    shapes = tuple(
        pltpu.VMEM((count, *((nx + 2, nz + 2 * GUARD, ny) if pad else (nx, nz, ny))), F32)
        for _, count, pad in RESIDENT
    )
    return pl.pallas_call(
        functools.partial(load_kernel, waits=len(after)),
        out_shape=shapes,
        in_specs=[SMEM] + [HBM] * 5 + [VMEM] * len(after),
        out_specs=(VMEM,) * len(shapes),
        scratch_shapes=[
            pltpu.SMEM(amps.shape, F32),
            pltpu.VMEM(receivers.shape, jnp.int32),
            pltpu.VMEM(recorded.shape, F32),
            pltpu.SemaphoreType.DMA((nf,)),
            pltpu.SemaphoreType.DMA,
            pltpu.SemaphoreType.DMA((3,)),
        ],
        compiler_params=PARAMS,
        cost_estimate=cost(nx * nz * ny, 150),
        name="load_fields",
    )(
        cell,
        *[in_hbm(x) for x in (amps, receivers, recorded, state, adjoint)],
        *[in_vmem(x) for x in after],
    )


def march_kernel(me_ref, *refs, n, spans, gathered, summed, waits):
    pieces = refs[: 2 * len(gathered)]
    refs = refs[len(pieces) + waits + len(RESIDENT) :]
    r = dict(zip(NAMES, refs))
    outs = refs[len(RESIDENT) :]
    st, q1, q2, eh, fr, adj, hits, seen, strain, model, grad, source = [r[name] for name in NAMES]
    _, nx, nz, ny = adj.shape
    piece = nz // n
    me = me_ref[0]

    def rows_of(rel):
        return pl.ds(pl.multiple_of((me ^ rel) * piece, piece), piece)

    for part, (low, high, rels) in enumerate(gathered):
        span = high - low
        near, core = pieces[2 * part : 2 * part + 2]

        def assemble(x, carry):
            for k in range(4):
                at = pl.ds((k * span + x) * piece, piece)
                for i, rel in enumerate(rels):
                    model[k, low + x, rows_of(rel), :] = near[i, at, :]
                    model[k, low + x, rows_of(rel ^ 1), :] = core[i, at, :]
            return carry

        lax.fori_loop(0, span, assemble, 0)

    lane = lax.broadcasted_iota(jnp.int32, (CHUNK, ny), 1)
    first, last = lane == 0, lane == ny - 1
    zero = jnp.zeros((CHUNK, ny), F32)
    chunk = CHUNK

    def at(ref, f, x, z, dx=0, dz=0):
        return ref[f, x + 1 + dx, pl.ds(GUARD + z + dz, chunk), :]

    def put(ref, f, x, z, value):
        ref[f, x + 1, pl.ds(GUARD + z, chunk), :] = value

    def ahead(f):
        return jnp.where(last, zero, pltpu.roll(f, ny - 1, 1))

    def behind(f):
        return jnp.where(first, zero, pltpu.roll(f, 1, 1))

    def fwd(ref, f, x, z, axis, here=None):
        here = at(ref, f, x, z) if here is None else here
        if axis == 0:
            return at(ref, f, x, z, dx=1) - here
        if axis == 1:
            return at(ref, f, x, z, dz=1) - here
        return ahead(here) - here

    def bwd(ref, f, x, z, axis, here=None):
        here = at(ref, f, x, z) if here is None else here
        if axis == 0:
            return here - at(ref, f, x, z, dx=-1)
        if axis == 1:
            return here - at(ref, f, x, z, dz=-1)
        return here - behind(here)

    def over_cells(number, body):
        begin, end = spans[number]

        def plane(x):
            for z in range(0, nz, chunk):
                body(x, z)

        def planes(i, carry):
            for x in range(UNROLL):
                plane(begin + i * UNROLL + x)
            return carry

        whole = (end - begin) // UNROLL
        if whole:
            lax.fori_loop(0, whole, planes, 0)
        for x in range(begin + whole * UNROLL, end):
            plane(x)

    def mod(k, x, z):
        return model[k, x, pl.ds(z, chunk), :]

    def forces(x, z):
        sxx, szz, syy, sxz, sxy, szy, p = [at(st, 6 + i, x, z) for i in range(7)]
        fx = fwd(st, 6, x, z, 0, sxx) + bwd(st, 9, x, z, 1, sxz) + bwd(st, 10, x, z, 2, sxy)
        fz = bwd(st, 9, x, z, 0, sxz) + fwd(st, 7, x, z, 1, szz) + bwd(st, 11, x, z, 2, szy)
        fy = bwd(st, 10, x, z, 0, sxy) + bwd(st, 11, x, z, 1, szy) + fwd(st, 8, x, z, 2, syy)
        g = [fwd(st, 12, x, z, d, p) for d in range(3)]
        return (fx, fz, fy), g

    def velocities(x, z, q_from, q_at, q_to):
        f, g = forces(x, z)
        damp = mod(3, x, z)
        for d in range(3):
            q = at(q_from, q_at + d, x, z)
            drag = g[d] + damp * q
            put(st, d, x, z, at(st, d, x, z) + (C1 * f[d] + C2 * drag))
            put(q_to, d, x, z, q - (C3 * drag + C2 * f[d]))

    def strains(x, z, q):
        vx, vz, vy = [at(st, i, x, z) for i in range(3)]
        exx = bwd(st, 0, x, z, 0, vx)
        ezz = bwd(st, 1, x, z, 1, vz)
        eyy = bwd(st, 2, x, z, 2, vy)
        dq = bwd(q, 0, x, z, 0) + bwd(q, 1, x, z, 1) + bwd(q, 2, x, z, 2)
        hxz = fwd(st, 0, x, z, 1, vx) + fwd(st, 1, x, z, 0, vz)
        hxy = fwd(st, 0, x, z, 2, vx) + fwd(st, 2, x, z, 0, vy)
        hzy = fwd(st, 1, x, z, 2, vz) + fwd(st, 2, x, z, 1, vy)
        dv = exx + ezz + eyy
        w = ALPHA * dv + dq
        return exx, ezz, eyy, hxz, hxy, hzy, dv, w

    def stresses(x, z):
        exx, ezz, eyy, hxz, hxy, hzy, dv, w = strains(x, z, q1)
        lame, shear, biot = [DT * mod(k, x, z) for k in range(3)]
        bw = biot * w
        bulk = lame * dv + ALPHA * bw
        shear2 = 2.0 * shear
        for i, e in enumerate((exx, ezz, eyy)):
            put(st, 6 + i, x, z, at(st, 6 + i, x, z) + (shear2 * e + bulk))
        for i, h in enumerate((hxz, hxy, hzy)):
            put(st, 9 + i, x, z, at(st, 9 + i, x, z) + shear * h)
        put(st, 12, x, z, at(st, 12, x, z) - bw + source[0, x, pl.ds(z, chunk), :])
        for i, e in enumerate((exx, ezz, eyy, hxz, hxy, hzy, w)):
            strain[i, x, pl.ds(z, chunk), :] = e

    def adj_at(f, x, z):
        return adj[f, x, pl.ds(z, chunk), :]

    def correlate(x, z, e, h, w, s, p, first_time):
        lame, shear, biot = [DT * mod(k, x, z) for k in range(3)]
        trace = s[0] + s[1] + s[2]
        dv = e[0] + e[1] + e[2]
        load = ALPHA * trace - p
        diag = s[0] * e[0] + s[1] * e[1] + s[2] * e[2]
        off = s[3] * h[0] + s[4] * h[1] + s[5] * h[2]
        for k, value in enumerate((trace * dv, 2.0 * diag + off, load * w)):
            value = DT * value
            if not first_time:
                value = grad[k, x, pl.ds(z, chunk), :] + value
            grad[k, x, pl.ds(z, chunk), :] = value
        t = biot * load
        bulk = lame * trace + ALPHA * t
        shear2 = 2.0 * shear
        for i in range(3):
            put(eh, i, x, z, shear2 * s[i] + bulk)
        for i in range(3):
            put(eh, 3 + i, x, z, shear * s[3 + i])
        put(eh, 6, x, z, t)

    def stress_back_2(x, z):
        exx, ezz, eyy, hxz, hxy, hzy, dv, w = strains(x, z, q2)
        final_p = at(st, 12, x, z) - DT * mod(2, x, z) * w
        s = [adj_at(6 + i, x, z) for i in range(6)]
        p = adj_at(12, x, z) + (hits[0, x, pl.ds(z, chunk), :] * final_p - seen[0, x, pl.ds(z, chunk), :])
        adj[12, x, pl.ds(z, chunk), :] = p
        correlate(x, z, (exx, ezz, eyy), (hxz, hxy, hzy), w, s, p, True)

    def velocity_bars(x, z, v, q):
        ex, ez, ey, hxz, hxy, hzy, t = [at(eh, i, x, z) for i in range(7)]
        vx = v[0] - (fwd(eh, 0, x, z, 0, ex) + bwd(eh, 3, x, z, 1, hxz) + bwd(eh, 4, x, z, 2, hxy))
        vz = v[1] - (bwd(eh, 3, x, z, 0, hxz) + fwd(eh, 1, x, z, 1, ez) + bwd(eh, 5, x, z, 2, hzy))
        vy = v[2] - (bwd(eh, 4, x, z, 0, hxy) + bwd(eh, 5, x, z, 1, hzy) + fwd(eh, 2, x, z, 2, ey))
        qs = [q[d] - fwd(eh, 6, x, z, d, t) for d in range(3)]
        return (vx, vz, vy), qs

    def velocity_back_2(x, z):
        v, q = velocity_bars(
            x, z, [adj_at(d, x, z) for d in range(3)], [adj_at(3 + d, x, z) for d in range(3)]
        )
        damp = mod(3, x, z)
        total = zero
        for d in range(3):
            r = C3 * q[d] - C2 * v[d]
            put(fr, d, x, z, C1 * v[d] - C2 * q[d])
            put(fr, 3 + d, x, z, r)
            total = total + at(q1, d, x, z) * r
            adj[d, x, pl.ds(z, chunk), :] = v[d]
            adj[3 + d, x, pl.ds(z, chunk), :] = q[d] - damp * r
        grad[3, x, pl.ds(z, chunk), :] = total

    def stress_back_1(x, z):
        fx, fz, fy = [at(fr, i, x, z) for i in range(3)]
        s = [
            adj_at(6, x, z) - bwd(fr, 0, x, z, 0, fx),
            adj_at(7, x, z) - bwd(fr, 1, x, z, 1, fz),
            adj_at(8, x, z) - bwd(fr, 2, x, z, 2, fy),
            adj_at(9, x, z) - (fwd(fr, 0, x, z, 1, fx) + fwd(fr, 1, x, z, 0, fz)),
            adj_at(10, x, z) - (fwd(fr, 0, x, z, 2, fx) + fwd(fr, 2, x, z, 0, fy)),
            adj_at(11, x, z) - (fwd(fr, 1, x, z, 2, fz) + fwd(fr, 2, x, z, 1, fy)),
        ]
        p = adj_at(12, x, z) + (
            bwd(fr, 3, x, z, 0) + bwd(fr, 4, x, z, 1) + bwd(fr, 5, x, z, 2)
        )
        e = [strain[i, x, pl.ds(z, chunk), :] for i in range(7)]
        correlate(x, z, e[0:3], e[3:6], e[6], s, p, False)

    def velocity_back_1(x, z):
        v, q = velocity_bars(
            x, z, [adj_at(d, x, z) for d in range(3)], [adj_at(3 + d, x, z) for d in range(3)]
        )
        total = grad[3, x, pl.ds(z, chunk), :]
        for d in range(3):
            total = total + at(st, 3 + d, x, z) * (C3 * q[d] - C2 * v[d])
        grad[3, x, pl.ds(z, chunk), :] = -total

    over_cells(0, lambda x, z: velocities(x, z, st, 3, q1))
    over_cells(1, stresses)

    over_cells(2, lambda x, z: velocities(x, z, q1, 0, q2))
    over_cells(3, stress_back_2)
    over_cells(4, velocity_back_2)
    over_cells(5, stress_back_1)
    over_cells(6, velocity_back_1)

    if summed:
        low, high, rels = summed
        span = high - low
        keep, send = outs

        def split(x, carry):
            for k in range(4):
                at = pl.ds((k * span + x) * piece, piece)
                for i, rel in enumerate(rels):
                    keep[i, at, :] = grad[k, low + x, rows_of(rel), :]
                    send[i, at, :] = grad[k, low + x, rows_of(rel ^ 1), :]
            return carry

        lax.fori_loop(0, span, split, 0)


def march(me, fields, n, spans, gathered=(), pieces=(), summed=None, after=()):
    _, nx, nz, ny = fields[NAMES.index("adj")].shape
    outs = [pltpu.VMEM(f.shape, F32) for f in fields]
    if summed:
        part = (n // 2, 4 * (summed[1] - summed[0]) * (nz // n), ny)
        outs += [pltpu.VMEM(part, F32)] * 2
    lead = 1 + len(pieces) + len(after)
    work = sum(end - begin for begin, end in spans)
    result = pl.pallas_call(
        functools.partial(
            march_kernel, n=n, spans=spans, gathered=gathered, summed=summed, waits=len(after)
        ),
        out_shape=tuple(outs),
        in_specs=[SMEM] + [VMEM] * (len(pieces) + len(after) + len(fields)),
        out_specs=(VMEM,) * len(outs),
        input_output_aliases={lead + i: i for i in range(len(fields))},
        compiler_params=PARAMS,
        cost_estimate=cost(work * nz * ny, 100),
        name="march",
    )(me, *[in_vmem(x) for x in (*pieces, *after, *fields)])
    return result[: len(fields)], result[len(fields) :]


def join(a, b, after=()):
    def kernel(a_ref, b_ref, *refs):
        out = refs[-1]
        out[: a.shape[0]] = a_ref[...]
        out[a.shape[0] :] = b_ref[...]

    return pl.pallas_call(
        kernel,
        out_shape=pltpu.VMEM((a.shape[0] + b.shape[0], *a.shape[1:]), F32),
        in_specs=[VMEM] * (2 + len(after)),
        out_specs=VMEM,
        compiler_params=PARAMS,
        cost_estimate=cost(2 * a.size, 1),
        name="join",
    )(*[in_vmem(x) for x in (a, b, *after)])


def add_halves(keep, came, after=()):
    half = keep.shape[0] // 2

    def kernel(a, b, *refs):
        low, high = refs[-2:]
        low[...] = a[:half] + b[:half]
        high[...] = a[half:] + b[half:]

    return pl.pallas_call(
        kernel,
        out_shape=(pltpu.VMEM((half, *keep.shape[1:]), F32),) * 2,
        in_specs=[VMEM] * (2 + len(after)),
        out_specs=(VMEM,) * 2,
        compiler_params=PARAMS,
        cost_estimate=cost(keep.size, 1),
        name="add_halves",
    )(*[in_vmem(x) for x in (keep, came, *after)])


def finish(terms, cuts, factor, shape, scale):
    _, nx, piece, ny = shape

    def kernel(*refs):
        factor_ref, out = refs[-2:]
        for part, (low, high) in enumerate(zip(cuts, cuts[1:])):
            for x in range(low, high):
                for k in range(4):
                    at = (k * (high - low) + x - low) * piece
                    at = slice(at, at + piece)
                    total = refs[2 * part][0, at, :] + refs[2 * part + 1][0, at, :]
                    out[k, x] = total * factor_ref[k, x] * scale

    flat = [in_vmem(t) for part in terms for t in part]
    return pl.pallas_call(
        kernel,
        out_shape=jax.ShapeDtypeStruct(shape, F32),
        in_specs=[VMEM] * (len(flat) + 1),
        out_specs=VMEM,
        compiler_params=PARAMS,
        name="finish",
    )(*flat, in_vmem(factor))


def partner(x, bit, n):
    return lax.ppermute(x, "shot", [(i, i ^ bit) for i in range(n)])


PASSES = 7


def per_device(
    forward_state,
    adjoint_state,
    source_amp,
    source_cell,
    receiver_cells,
    recorded,
    material,
    cell_class,
    class_factors,
):
    n = lax.axis_size("shot")
    me = lax.axis_index("shot").reshape(1)
    nx = material.shape[1]
    along_z = [b for b in (4, 8, 16, 32, 64, 128) if b < n]

    factor, *owns = own_model(me, class_factors, cell_class, material, 2)
    ways = ([2, *along_z[::-1]], [*along_z[::-1], 2])
    data, rels = list(owns), [[0], [0]]
    fields, token = None, ()
    for step in range(len(ways[0])):
        came = [partner(d, way[step], n) for d, way in zip(data, ways)]
        if step == len(ways[0]) - 1:
            fields = load_fields(
                source_cell,
                source_amp,
                receiver_cells,
                recorded,
                forward_state[0],
                adjoint_state[0],
                data,
            )
            token = (fields[NAMES.index("hits")],)
        data = [join(d, c, token) for d, c in zip(data, came)]
        rels = [[*r, *[i ^ way[step] for i in r]] for r, way in zip(rels, ways)]
    pieces = [p for d in data for p in (d, partner(d, 1, n))]
    gathered = [(0, nx // 2, rels[0]), (nx // 2, nx, rels[1])]

    backs = ([2, *along_z], [*along_z, 2])
    cuts = [0, nx * 5 // 8, nx]
    done = [0] * PASSES
    terms = []
    for low, high, back in zip(cuts, cuts[1:], backs):
        rels = [0]
        for b in back[::-1]:
            rels = [*rels, *[i ^ b for i in rels]]
        limits = [min(nx, high + PASSES - 1 - p) for p in range(PASSES)]
        spans = tuple((d, max(d, limit)) for d, limit in zip(done, limits))
        done = [end for _, end in spans]
        fields, (keep, send) = march(me, fields, n, spans, gathered, pieces, (low, high, rels))
        gathered, pieces = (), ()
        came = partner(send, 1, n)
        for b in back:
            keep, send = add_halves(keep, came)
            came = partner(send, b, n)
        terms.append((keep, came))
    scale = 1.0 / float(forward_state.shape[0] * n) ** 0.5
    return finish(terms, cuts, factor, material.shape, scale)


def solution(mesh):
    placed = (
        P(("groups", "shot"), None, None, None, None),
        P(("groups", "shot"), None, None, None, None),
        P(("groups", "shot"), None),
        P(("groups", "shot")),
        P(("groups", "shot"), None),
        P(("groups", "shot"), None),
        P(None, "groups", "shot", None),
        P("groups", None, None),
        P(),
    )
    return jax.shard_map(
        per_device,
        mesh=mesh,
        in_specs=placed,
        out_specs=P(None, "groups", "shot", None),
        check_vma=False,
    )
```
